256 devices in a mesh: pair: 16 (over x, z_lo, core), pw: 16 (over z_hi, y).
Axes of the slice: x: 4, y: 4, z: 8 (z_hi: 4, z_lo: 2; z = z_hi * 2 + z_lo), core: 2. Of those that a mesh axis runs over, the one named last changes fastest.
Arguments:
- pair_products: bfloat16 [32768, 8192], P('pw', 'pair'), may hold values from -40 to 40
- basis: bfloat16 [32768, 1024], P('pw'), may hold values from -0.046875 to 0.046875
- val_energy: float32 [128], replicated, may hold values from -0.05 to -0.001
- cond_energy: float32 [128], replicated, may hold values from 0.001 to 40
- frequencies: float32 [8], replicated, may hold values from 0.002 to 20
- valence_index: int32 [8192], P('pair'), may hold values from 0 to 127
- conduction_index: int32 [8192], P('pair'), may hold values from 0 to 127
Outputs:
- response: float32 [8, 1024, 1024], P(None, 'pw', 'pair')
The draws below stay inside these ranges and needn't reach their ends.
All inputs are finite; a program needn't handle non-finite values.
Results may differ from the reference program's by a relative error of at most 0.0055.
Values may be sent and summed in bfloat16 or wider, within the bound.
A program may use at most 64 MiB of HBM per device.

```python
import math
import jax
import jax.numpy as jnp
from jax import lax

NPW = 32768
NB = 1024
NW = 8
NV = 128
NC = 128
GROUPS = 2
PAIRS = 8192
N_PAIR = 16


def band_tables(key):
    valence = jax.random.randint(jax.random.fold_in(key, 101), (PAIRS,), 0, NV).astype(jnp.int32)
    conduction = jax.random.randint(jax.random.fold_in(key, 102), (PAIRS,), 0, NC).astype(jnp.int32)
    depths = jnp.exp(jax.random.uniform(jax.random.fold_in(key, 103), (NV,), jnp.float32, math.log(0.001), math.log(0.05)))
    heights = jnp.exp(jax.random.uniform(jax.random.fold_in(key, 104), (NC,), jnp.float32, math.log(0.001), math.log(40.0)))
    lower = -jnp.clip(depths, 0.001, 0.05)
    upper = jnp.clip(heights, 0.001, 40.0)
    return (valence, conduction, lower, upper)


def draw_valence_index(key, part):
    return band_tables(key)[0]


def draw_conduction_index(key, part):
    return band_tables(key)[1]


def draw_val_energy(key, part):
    return band_tables(key)[2]


def draw_cond_energy(key, part):
    return band_tables(key)[3]


def draw_pair_products(key, part):
    valence, conduction, lower, upper = band_tables(key)
    energy_gap = upper[conduction] - lower[valence]
    column_scale = jnp.sqrt(energy_gap)
    values = jnp.clip(jax.random.normal(jax.random.fold_in(key, 105), (NPW, PAIRS), jnp.float32), -6.0, 6.0)
    return jnp.clip(values * column_scale[None, :], -40.0, 40.0).astype(jnp.bfloat16)


def draw_frequencies(key, part):
    shifts = jax.random.uniform(jax.random.fold_in(key, 201), (NW,), jnp.float32, 0.1, 0.9)
    order = jax.random.permutation(jax.random.fold_in(key, 202), NW).astype(jnp.float32)
    low_end = math.log(0.002)
    high_end = math.log(20.0)
    levels = (order + shifts) * ((high_end - low_end) / NW) + low_end
    return jnp.clip(jnp.exp(levels), 0.002, 20.0)


def raised(result, own_key, source, target, parts, factor):
    owner, partner = [(jnp.arange(result.shape[dim]) // (result.shape[dim] // parts)).reshape([-1 if axis == dim else 1 for axis in range(result.ndim)]) for dim in (source, target)]
    chosen = jax.random.permutation(own_key, parts)[partner]
    strong = (owner == chosen) | (owner == (partner + parts // 2) % parts)
    return jnp.where(strong, factor * result, result)


def steps_of(rng, extent, split, least, high):
    loudness, own = 1.0, jax.random.fold_in(rng, 6)
    for dim, shards_of in split:
        steps = jnp.exp(jax.random.uniform(jax.random.fold_in(own, dim), (shards_of,), jnp.float32, least / len(split), high / len(split)))
        loudness = loudness * jnp.repeat(steps, extent[dim] // shards_of).reshape([-1 if axis == dim else 1 for axis in range(len(extent))])
    return loudness


def heavy_noise(own_key, extent, spread, reach, pieces, heavy, kind=jnp.bfloat16):
    drawn = spread * jax.random.normal(own_key, extent, jnp.float32)
    if pieces:
        drawn = drawn * steps_of(own_key, extent, pieces, -0.22, 0.18)
    return jnp.clip(raised(drawn, jax.random.fold_in(own_key, 3), *heavy), -reach, reach).astype(kind)


def setup_inputs(seed: int = 0) -> dict:
    splits = jax.random.split(jax.random.key(seed), 8)
    pair_products = draw_pair_products(jax.random.fold_in(splits[7], 71), 0)
    basis = heavy_noise(splits[1], (NPW, NB), NPW ** -0.5, 0.046875, ((0, 16),), (0, 1, 16, 2.0))
    val_energy = draw_val_energy(jax.random.fold_in(splits[7], 71), 0)
    cond_energy = draw_cond_energy(jax.random.fold_in(splits[7], 71), 0)
    frequencies = draw_frequencies(jax.random.fold_in(splits[7], 71), 0)
    valence_index = draw_valence_index(jax.random.fold_in(splits[7], 71), 0)
    conduction_index = draw_conduction_index(jax.random.fold_in(splits[7], 71), 0)
    return dict(pair_products=pair_products, basis=basis, val_energy=val_energy, cond_energy=cond_energy, frequencies=frequencies, valence_index=valence_index, conduction_index=conduction_index)


def reference(pair_products, basis, val_energy, cond_energy, frequencies, valence_index, conduction_index):
    energy_gap = cond_energy[conduction_index] - val_energy[valence_index]
    weights = -4.0 * energy_gap[None, :] / (energy_gap[None, :] ** 2 + frequencies[:, None] ** 2) / PAIRS
    block_size = PAIRS // (N_PAIR * GROUPS)

    def add_block(gram_total, position):
        offset = (position * block_size).astype(jnp.int32)
        pair_block = lax.dynamic_slice_in_dim(pair_products, offset, block_size, 1)
        projected = lax.dot_general(basis, pair_block, (((0,), (0,)), ((), ())), preferred_element_type=jnp.float32).astype(jnp.bfloat16)
        weight_block = lax.dynamic_slice_in_dim(weights, offset, block_size, 1)
        weighted = (weight_block[:, None, :] * projected.astype(jnp.float32)[None]).astype(jnp.bfloat16)
        gram_total = gram_total + jnp.einsum("kpc,nc->kpn", weighted.astype(jnp.float32), projected.astype(jnp.float32))
        return gram_total, None

    start_total = jnp.zeros((NW, NB, NB), jnp.float32)
    response, _ = lax.scan(add_block, start_total, jnp.arange(N_PAIR * GROUPS, dtype=jnp.int32))
    return response
```

```python
import functools

import jax
import jax.numpy as jnp
from jax import lax
from jax.experimental import pallas as pl
from jax.experimental.pallas import tpu as pltpu
from jax.sharding import PartitionSpec as P

F32 = jnp.float32
BF16 = jnp.bfloat16
MESH = pl.DeviceIdType.MESH
CHUNKS = 4
HALVES = 2


def kernel(
    pairs_total,
    pp_hbm,
    basis_hbm,
    val_ref,
    cond_ref,
    freq_ref,
    vidx_ref,
    cidx_ref,
    out_ref,
    basis_v,
    pp_v,
    psend,
    yrecv,
    zsend,
    zrecv,
    mbuf,
    nbuf,
    wbuf,
    acc,
    csend,
    crecv,
    basis_sem,
    pp_sem,
    y_ss,
    y_rs,
    z_ss,
    z_rs,
    m_ss,
    m_rs,
    n_ss,
    n_rs,
    r_ss,
    r_rs,
    w_ss,
    w_rs,
    c_ss,
    c_rs,
):
    pair, pw = lax.axis_index("pair"), lax.axis_index("pw")
    x, zl, cc = pair // 4, (pair // 2) % 2, pair % 2
    zh, y = pw // 4, pw % 4
    y_hi, y_lo = y // 2, y % 2

    def dev(x=x, zl=zl, cc=cc, zh=zh, y=y):
        return {"pair": x * 4 + zl * 2 + cc, "pw": zh * 4 + y}

    def basis_load(zb):
        return pltpu.make_async_copy(
            basis_hbm.at[:, pl.ds(pl.multiple_of(zb * 256, 256), 256)],
            basis_v.at[zb],
            basis_sem.at[zb],
        )

    def pp_load(h):
        return pltpu.make_async_copy(
            pp_hbm.at[:, pl.ds(h * 256, 256)], pp_v.at[h], pp_sem.at[h]
        )

    pp_load(0).start()
    for zb in range(4):
        basis_load(zb).start()
    pp_load(1).start()

    own_n = y_hi == cc
    own_c = jnp.logical_and(y == 2 * zl + cc, y_hi == cc)
    barrier = pltpu.get_barrier_semaphore()

    def greet(device):
        pl.semaphore_signal(barrier, inc=1, device_id=device, device_id_type=MESH)

    for d in range(1, 4):
        greet(dev(y=(y + 4 - d) % 4))
        greet(dev(zh=(zh + 4 - d) % 4))
    greet(dev(cc=1 - cc))
    for j in range(2):
        for pc in range(2):
            mine = jnp.logical_and(own_n, jnp.logical_and(y_lo == j, cc == pc))

            @pl.when(jnp.logical_not(mine))
            def _():
                greet(dev(y=2 * cc + j, cc=pc))

    for slot in range(8):
        source = dev(
            x=(x + 4 - slot // 2) % 4, zl=(zl + slot % 2) % 2, y=2 * zl + cc, cc=y_hi
        )
        if slot == 0:

            @pl.when(jnp.logical_not(own_c))
            def _():
                greet(source)
        else:
            greet(source)
    expected = 19 - jnp.where(own_n, 1, 0) - jnp.where(own_c, 1, 0)

    def y_copy(c, d):
        return pltpu.make_async_remote_copy(
            src_ref=psend.at[c, (y + d) % 4],
            dst_ref=yrecv.at[c, d - 1],
            send_sem=y_ss.at[c, d - 1],
            recv_sem=y_rs.at[c, d - 1],
            device_id=dev(y=(y + d) % 4),
            device_id_type=MESH,
        )

    def z_copy(c, d):
        return pltpu.make_async_remote_copy(
            src_ref=zsend.at[c, (zh + d) % 4],
            dst_ref=zrecv.at[c, d - 1],
            send_sem=z_ss.at[c, d - 1],
            recv_sem=z_rs.at[c, d - 1],
            device_id=dev(zh=(zh + d) % 4),
            device_id_type=MESH,
        )

    def m_copy(c, d):
        return pltpu.make_async_remote_copy(
            src_ref=mbuf.at[c, cc, zh],
            dst_ref=mbuf.at[c, cc, zh],
            send_sem=m_ss.at[c, d - 1],
            recv_sem=m_rs.at[c, d - 1],
            device_id=dev(zh=(zh + d) % 4),
            device_id_type=MESH,
        )

    def n_copy(c, d):
        return pltpu.make_async_remote_copy(
            src_ref=mbuf.at[c, cc, zh],
            dst_ref=nbuf.at[c, y_lo, cc],
            send_sem=n_ss.at[c, d],
            recv_sem=n_rs.at[c, y_lo * 2 + cc],
            device_id=dev(y=(y + d) % 4, cc=y_hi),
            device_id_type=MESH,
        )

    def n_arrival(c, j, pc):
        return pltpu.make_async_remote_copy(
            src_ref=mbuf.at[c, cc, zh],
            dst_ref=nbuf.at[c, j, pc],
            send_sem=n_ss.at[c, 0],
            recv_sem=n_rs.at[c, j * 2 + pc],
            device_id=dev(cc=1 - cc),
            device_id_type=MESH,
        )

    def relay(c):
        return pltpu.make_async_remote_copy(
            src_ref=mbuf.at[c, cc],
            dst_ref=mbuf.at[c, cc],
            send_sem=r_ss.at[c],
            recv_sem=r_rs.at[c],
            device_id=dev(cc=1 - cc),
            device_id_type=MESH,
        )

    w_copy = pltpu.make_async_remote_copy(
        src_ref=wbuf.at[cc],
        dst_ref=wbuf.at[cc],
        send_sem=w_ss,
        recv_sem=w_rs,
        device_id=dev(cc=1 - cc),
        device_id_type=MESH,
    )

    def c_copy(j, block):
        slot = ((block + 4 - x) % 4) * 2 + (y_hi + zl) % 2
        return pltpu.make_async_remote_copy(
            src_ref=csend.at[j, block],
            dst_ref=crecv.at[slot],
            send_sem=c_ss.at[j, block],
            recv_sem=c_rs.at[slot],
            device_id=dev(y=2 * cc + j, x=block, zl=y_hi, cc=y_lo),
            device_id_type=MESH,
        )

    def c_arrival(slot):
        return pltpu.make_async_remote_copy(
            src_ref=csend.at[0, 0],
            dst_ref=crecv.at[slot],
            send_sem=c_ss.at[0, 0],
            recv_sem=c_rs.at[slot],
            device_id=dev(cc=1 - cc),
            device_id_type=MESH,
        )

    def project(h):
        pp_load(h).wait()

        def rows(zb, carry):
            if h == 0:
                basis_load(zb).wait()
            block = lax.dot_general(
                basis_v[zb],
                pp_v[h],
                (((0,), (0,)), ((), ())),
                preferred_element_type=F32,
            )
            block = block.astype(BF16).reshape(4, 64, 256)
            psend[2 * h, :, zb] = block[:, :, :128]
            psend[2 * h + 1, :, zb] = block[:, :, 128:]
            return carry

        lax.fori_loop(0, 4, rows, 0)

    def send_y(c):
        for d in (2, 1, 3):
            y_copy(c, d).start()

    def make_weights():
        levels = lax.broadcasted_iota(jnp.int32, (128, 512), 0)

        def lookup(index, table):
            column = jnp.transpose(jnp.broadcast_to(table, (128, 128)))[:, :1]
            return jnp.sum(jnp.where(levels == index, column, 0.0), axis=0, keepdims=True)

        gap = lookup(cidx_ref[...], cond_ref[...]) - lookup(vidx_ref[...], val_ref[...])
        for k in range(8):
            freq = freq_ref[k]
            weight = -4.0 * gap / (gap * gap + freq * freq) / pairs_total
            for c in range(CHUNKS):
                wbuf[cc, c, k : k + 1, :] = weight[:, c * 128 : (c + 1) * 128]

    def stage_y(c):
        for d in range(1, 4):
            y_copy(c, d).wait_recv()
        total = psend[c, y].astype(F32)
        for d in range(3):
            total += yrecv[c, d].astype(F32)
        zsend[c] = total.astype(BF16)
        for d in (2, 1, 3):
            z_copy(c, d).start()

    def stage_z(c):
        for d in range(1, 4):
            z_copy(c, d).wait_recv()
        total = zsend[c, zh].astype(F32)
        for d in range(3):
            total += zrecv[c, d].astype(F32)
        own = total.astype(BF16)
        mbuf[c, cc, zh] = own

        @pl.when(own_n)
        def _():
            nbuf[c, y_lo, cc] = own

        for d in (2, 1, 3):
            m_copy(c, d).start()
        for d in (2, 1, 3):
            n_copy(c, d).start()

        @pl.when(jnp.logical_not(own_n))
        def _():
            n_copy(c, 0).start()

    def stage_relay(c):
        for d in range(1, 4):
            m_copy(c, d).wait_recv()
        relay(c).start()

    def stage_response(c):
        if c == 0:
            w_copy.wait_recv()
        for j in range(2):
            for pc in range(2):
                mine = jnp.logical_and(own_n, jnp.logical_and(y_lo == j, cc == pc))

                @pl.when(jnp.logical_not(mine))
                def _():
                    n_arrival(c, j, pc).wait_recv()

        relay(c).wait_recv()
        right = jnp.concatenate([mbuf[c, pc].reshape(256, 128) for pc in range(2)], axis=1)
        for j in range(2):
            left = jnp.concatenate(
                [
                    (wbuf[pc, c][:, None, :] * nbuf[c, j, pc].astype(F32)[None])
                    .astype(BF16)
                    .reshape(512, 128)
                    for pc in range(2)
                ],
                axis=1,
            )
            part = lax.dot_general(
                left, right, (((1,), (1,)), ((), ())), preferred_element_type=F32
            )
            if c == 0:
                acc[j] = part
            else:
                acc[j] += part

    def send_tiles(j):
        rows = acc[j].reshape(8, 64, 256)
        for block in range(4):
            lanes = rows[:, :, block * 64 : (block + 1) * 64]
            tile = jnp.concatenate([lanes[:, :32], lanes[:, 32:]], axis=2).astype(BF16)
            csend[j, block] = tile
            mine = jnp.logical_and(own_c, jnp.logical_and(y_lo == j, x == block))

            @pl.when(mine)
            def _():
                crecv[0] = tile

            @pl.when(jnp.logical_not(mine))
            def _():
                c_copy(j, block).start()

    project(0)
    pl.semaphore_wait(barrier, expected)
    send_y(0)
    send_y(1)
    project(1)
    send_y(2)
    send_y(3)
    make_weights()
    w_copy.start()
    for t in range(CHUNKS + 3):
        if t < CHUNKS:
            stage_y(t)
        if 0 <= t - 1 < CHUNKS:
            stage_z(t - 1)
        if 0 <= t - 2 < CHUNKS:
            stage_relay(t - 2)
        if 0 <= t - 3 < CHUNKS:
            stage_response(t - 3)
    for j in range(2):
        send_tiles(j)

    for c in range(CHUNKS):
        for d in range(1, 4):
            y_copy(c, d).wait_send()
            z_copy(c, d).wait_send()
            m_copy(c, d).wait_send()
            n_copy(c, d).wait_send()

        @pl.when(jnp.logical_not(own_n))
        def _():
            n_copy(c, 0).wait_send()

        relay(c).wait_send()
    w_copy.wait_send()

    @pl.when(jnp.logical_not(own_c))
    def _():
        c_arrival(0).wait_recv()

    total = crecv[0].astype(F32)
    for slot in range(1, 8):
        c_arrival(slot).wait_recv()
        total += crecv[slot].astype(F32)
    out_ref[:, :32, :] = total[:, :, :64]
    out_ref[:, 32:, :] = total[:, :, 64:]
    for j in range(2):
        for block in range(4):
            mine = jnp.logical_and(own_c, jnp.logical_and(y_lo == j, x == block))

            @pl.when(jnp.logical_not(mine))
            def _():
                c_copy(j, block).wait_send()


def per_device(
    pair_products, basis, val_energy, cond_energy, frequencies, valence_index, conduction_index
):
    pairs_total = pair_products.shape[1] * lax.axis_size("pair")
    vmem = pl.BlockSpec(memory_space=pltpu.VMEM)
    smem = pl.BlockSpec(memory_space=pltpu.SMEM)
    hbm = pl.BlockSpec(memory_space=pl.ANY)
    dma = pltpu.SemaphoreType.DMA
    return pl.pallas_call(
        functools.partial(kernel, pairs_total),
        out_shape=jax.ShapeDtypeStruct((8, 64, 64), F32),
        in_specs=[hbm, hbm, vmem, vmem, smem, vmem, vmem],
        out_specs=vmem,
        scratch_shapes=[
            pltpu.VMEM((4, 2048, 256), BF16),
            pltpu.VMEM((HALVES, 2048, 256), BF16),
            pltpu.VMEM((CHUNKS, 4, 4, 64, 128), BF16),
            pltpu.VMEM((CHUNKS, 3, 4, 64, 128), BF16),
            pltpu.VMEM((CHUNKS, 4, 64, 128), BF16),
            pltpu.VMEM((CHUNKS, 3, 64, 128), BF16),
            pltpu.VMEM((CHUNKS, 2, 4, 64, 128), BF16),
            pltpu.VMEM((CHUNKS, 2, 2, 64, 128), BF16),
            pltpu.VMEM((2, CHUNKS, 8, 128), F32),
            pltpu.VMEM((2, 512, 256), F32),
            pltpu.VMEM((2, 4, 8, 32, 128), BF16),
            pltpu.VMEM((8, 8, 32, 128), BF16),
            dma((4,)),
            dma((HALVES,)),
            dma((CHUNKS, 3)),
            dma((CHUNKS, 3)),
            dma((CHUNKS, 3)),
            dma((CHUNKS, 3)),
            dma((CHUNKS, 3)),
            dma((CHUNKS, 3)),
            dma((CHUNKS, 4)),
            dma((CHUNKS, 4)),
            dma((CHUNKS,)),
            dma((CHUNKS,)),
            dma(()),
            dma(()),
            dma((2, 4)),
            dma((8,)),
        ],
        compiler_params=pltpu.CompilerParams(
            collective_id=0, has_side_effects=True, vmem_limit_bytes=48 * 2**20
        ),
    )(
        pair_products,
        basis,
        val_energy.reshape(1, -1),
        cond_energy.reshape(1, -1),
        frequencies,
        valence_index.reshape(1, -1),
        conduction_index.reshape(1, -1),
    )


def solution(mesh):
    placed = (P("pw", "pair"), P("pw", None), P(), P(), P(), P("pair"), P("pair"))
    return jax.shard_map(
        per_device, mesh=mesh, in_specs=placed, out_specs=P(None, "pw", "pair"), check_vma=False
    )
```

```python
import functools

import jax
import jax.numpy as jnp
from jax import lax
from jax.experimental import pallas as pl
from jax.experimental.pallas import tpu as pltpu
from jax.sharding import PartitionSpec as P

F32 = jnp.float32
BF16 = jnp.bfloat16
MESH = pl.DeviceIdType.MESH
CHUNKS = 4
HALVES = 2


def kernel(
    pairs_total,
    pp_hbm,
    basis_hbm,
    val_hbm,
    cond_hbm,
    freq_hbm,
    vidx_hbm,
    cidx_hbm,
    out_ref,
    val_ref,
    cond_ref,
    freq_ref,
    vidx_ref,
    cidx_ref,
    small_sem,
    basis_v,
    pp_v,
    psend,
    yrecv,
    zsend,
    zrecv,
    mbuf,
    nbuf,
    wbuf,
    acc,
    csend,
    xrecv,
    fsend,
    frecv,
    basis_sem,
    pp_sem,
    y_ss,
    y_rs,
    z_ss,
    z_rs,
    m_ss,
    m_rs,
    n_ss,
    n_rs,
    r_ss,
    r_rs,
    w_ss,
    w_rs,
    x_ss,
    x_rs,
    f_ss,
    f_rs,
):
    pair, pw = lax.axis_index("pair"), lax.axis_index("pw")
    x, zl, cc = pair // 4, (pair // 2) % 2, pair % 2
    zh, y = pw // 4, pw % 4
    y_hi, y_lo = y // 2, y % 2

    def dev(x=x, zl=zl, cc=cc, zh=zh, y=y):
        return {"pair": x * 4 + zl * 2 + cc, "pw": zh * 4 + y}

    def basis_load(zb):
        return pltpu.make_async_copy(
            basis_hbm.at[:, pl.ds(pl.multiple_of(zb * 256, 256), 256)],
            basis_v.at[zb],
            basis_sem.at[zb],
        )

    def pp_load(h):
        return pltpu.make_async_copy(
            pp_hbm.at[:, pl.ds(h * 256, 256)], pp_v.at[h], pp_sem.at[h]
        )

    pp_load(0).start()
    for zb in range(4):
        basis_load(zb).start()
    pp_load(1).start()
    small_loads = [
        pltpu.make_async_copy(source, target, small_sem.at[i])
        for i, (source, target) in enumerate(
            [
                (val_hbm, val_ref),
                (cond_hbm, cond_ref),
                (freq_hbm, freq_ref),
                (vidx_hbm, vidx_ref),
                (cidx_hbm, cidx_ref),
            ]
        )
    ]
    for load in small_loads:
        load.start()

    own_n = y_hi == cc
    own_c = jnp.logical_and(y == 2 * zl + cc, y_hi == cc)
    barrier = pltpu.get_barrier_semaphore()

    def greet(device):
        pl.semaphore_signal(barrier, inc=1, device_id=device, device_id_type=MESH)

    for d in range(1, 4):
        greet(dev(y=(y + 4 - d) % 4))
        greet(dev(zh=(zh + 4 - d) % 4))
        greet(dev(x=(x + 4 - d) % 4))
    greet(dev(cc=1 - cc))
    for j in range(2):
        for pc in range(2):
            mine = jnp.logical_and(own_n, jnp.logical_and(y_lo == j, cc == pc))

            @pl.when(jnp.logical_not(mine))
            def _():
                greet(dev(y=2 * cc + j, cc=pc))

    greet(dev(zl=1 - zl, y=2 * zl + cc, cc=y_hi))

    @pl.when(jnp.logical_not(own_c))
    def _():
        greet(dev(y=2 * zl + cc, cc=y_hi))

    expected = 16 - jnp.where(own_n, 1, 0) - jnp.where(own_c, 1, 0)

    def y_copy(c, d):
        return pltpu.make_async_remote_copy(
            src_ref=psend.at[c, (y + d) % 4],
            dst_ref=yrecv.at[c, d - 1],
            send_sem=y_ss.at[c, d - 1],
            recv_sem=y_rs.at[c, d - 1],
            device_id=dev(y=(y + d) % 4),
            device_id_type=MESH,
        )

    def z_copy(c, d):
        return pltpu.make_async_remote_copy(
            src_ref=zsend.at[c, (zh + d) % 4],
            dst_ref=zrecv.at[c, d - 1],
            send_sem=z_ss.at[c, d - 1],
            recv_sem=z_rs.at[c, d - 1],
            device_id=dev(zh=(zh + d) % 4),
            device_id_type=MESH,
        )

    def m_copy(c, d):
        return pltpu.make_async_remote_copy(
            src_ref=mbuf.at[c, cc, zh],
            dst_ref=mbuf.at[c, cc, zh],
            send_sem=m_ss.at[c, d - 1],
            recv_sem=m_rs.at[c, d - 1],
            device_id=dev(zh=(zh + d) % 4),
            device_id_type=MESH,
        )

    def n_copy(c, d):
        return pltpu.make_async_remote_copy(
            src_ref=mbuf.at[c, cc, zh],
            dst_ref=nbuf.at[c, y_lo, cc],
            send_sem=n_ss.at[c, d],
            recv_sem=n_rs.at[c, y_lo * 2 + cc],
            device_id=dev(y=(y + d) % 4, cc=y_hi),
            device_id_type=MESH,
        )

    def n_arrival(c, j, pc):
        return pltpu.make_async_remote_copy(
            src_ref=mbuf.at[c, cc, zh],
            dst_ref=nbuf.at[c, j, pc],
            send_sem=n_ss.at[c, 0],
            recv_sem=n_rs.at[c, j * 2 + pc],
            device_id=dev(cc=1 - cc),
            device_id_type=MESH,
        )

    def relay(c):
        return pltpu.make_async_remote_copy(
            src_ref=mbuf.at[c, cc],
            dst_ref=mbuf.at[c, cc],
            send_sem=r_ss.at[c],
            recv_sem=r_rs.at[c],
            device_id=dev(cc=1 - cc),
            device_id_type=MESH,
        )

    w_copy = pltpu.make_async_remote_copy(
        src_ref=wbuf.at[cc],
        dst_ref=wbuf.at[cc],
        send_sem=w_ss,
        recv_sem=w_rs,
        device_id=dev(cc=1 - cc),
        device_id_type=MESH,
    )

    def x_copy(j, d):
        return pltpu.make_async_remote_copy(
            src_ref=csend.at[j, (x + d) % 4],
            dst_ref=xrecv.at[j, d - 1],
            send_sem=x_ss.at[j, d - 1],
            recv_sem=x_rs.at[j, d - 1],
            device_id=dev(x=(x + d) % 4),
            device_id_type=MESH,
        )

    def f_copy(j):
        slot = (y_hi + zl) % 2
        return pltpu.make_async_remote_copy(
            src_ref=fsend.at[j],
            dst_ref=frecv.at[slot],
            send_sem=f_ss.at[j],
            recv_sem=f_rs.at[slot],
            device_id=dev(y=2 * cc + j, zl=y_hi, cc=y_lo),
            device_id_type=MESH,
        )

    def f_arrival(slot):
        return pltpu.make_async_remote_copy(
            src_ref=fsend.at[0],
            dst_ref=frecv.at[slot],
            send_sem=f_ss.at[0],
            recv_sem=f_rs.at[slot],
            device_id=dev(cc=1 - cc),
            device_id_type=MESH,
        )

    def project(h):
        pp_load(h).wait()

        def rows(zb, carry):
            if h == 0:
                basis_load(zb).wait()
            block = lax.dot_general(
                basis_v[zb],
                pp_v[h],
                (((0,), (0,)), ((), ())),
                preferred_element_type=F32,
            )
            block = block.astype(BF16).reshape(4, 64, 256)
            psend[2 * h, :, zb] = block[:, :, :128]
            psend[2 * h + 1, :, zb] = block[:, :, 128:]
            return carry

        lax.fori_loop(0, 4, rows, 0)

    def send_y(c):
        for d in (2, 1, 3):
            y_copy(c, d).start()

    def make_weights():
        for load in small_loads:
            load.wait()
        levels = lax.broadcasted_iota(jnp.int32, (128, 512), 0)

        def lookup(index, table):
            column = jnp.transpose(jnp.broadcast_to(table, (128, 128)))[:, :1]
            return jnp.sum(jnp.where(levels == index, column, 0.0), axis=0, keepdims=True)

        gap = lookup(cidx_ref[...], cond_ref[...]) - lookup(vidx_ref[...], val_ref[...])
        for k in range(8):
            freq = freq_ref[k]
            weight = -4.0 * gap / (gap * gap + freq * freq) / pairs_total
            for c in range(CHUNKS):
                wbuf[cc, c, k : k + 1, :] = weight[:, c * 128 : (c + 1) * 128]

    def stage_y(c):
        for d in range(1, 4):
            y_copy(c, d).wait_recv()
        total = psend[c, y].astype(F32)
        for d in range(3):
            total += yrecv[c, d].astype(F32)
        zsend[c] = total.astype(BF16)
        for d in (2, 1, 3):
            z_copy(c, d).start()

    def stage_z(c):
        for d in range(1, 4):
            z_copy(c, d).wait_recv()
        total = zsend[c, zh].astype(F32)
        for d in range(3):
            total += zrecv[c, d].astype(F32)
        own = total.astype(BF16)
        mbuf[c, cc, zh] = own

        @pl.when(own_n)
        def _():
            nbuf[c, y_lo, cc] = own

        for d in (2, 1, 3):
            m_copy(c, d).start()
        for d in (2, 1, 3):
            n_copy(c, d).start()

        @pl.when(jnp.logical_not(own_n))
        def _():
            n_copy(c, 0).start()

    def stage_relay(c):
        for d in range(1, 4):
            m_copy(c, d).wait_recv()
        relay(c).start()

    def stage_response(c):
        if c == 0:
            w_copy.wait_recv()
        for j in range(2):
            for pc in range(2):
                mine = jnp.logical_and(own_n, jnp.logical_and(y_lo == j, cc == pc))

                @pl.when(jnp.logical_not(mine))
                def _():
                    n_arrival(c, j, pc).wait_recv()

        relay(c).wait_recv()
        right = jnp.concatenate([mbuf[c, pc].reshape(256, 128) for pc in range(2)], axis=1)
        for j in range(2):
            left = jnp.concatenate(
                [
                    (wbuf[pc, c][:, None, :] * nbuf[c, j, pc].astype(F32)[None])
                    .astype(BF16)
                    .reshape(512, 128)
                    for pc in range(2)
                ],
                axis=1,
            )
            part = lax.dot_general(
                left, right, (((1,), (1,)), ((), ())), preferred_element_type=F32
            )
            if c == 0:
                acc[j] = part
            else:
                acc[j] += part

    def send_tiles(j):
        rows = acc[j].reshape(8, 64, 256)
        for block in range(4):
            lanes = rows[:, :, block * 64 : (block + 1) * 64]
            tile = jnp.concatenate([lanes[:, :32], lanes[:, 32:]], axis=2).astype(BF16)
            csend[j, block] = tile
        for d in (2, 1, 3):
            x_copy(j, d).start()

    def stage_x(j):
        for d in range(1, 4):
            x_copy(j, d).wait_recv()
        total = csend[j, x].astype(F32)
        for d in range(3):
            total += xrecv[j, d].astype(F32)
        tile = total.astype(BF16)
        fsend[j] = tile
        mine = jnp.logical_and(own_c, y_lo == j)

        @pl.when(mine)
        def _():
            frecv[0] = tile

        @pl.when(jnp.logical_not(mine))
        def _():
            f_copy(j).start()

    project(0)
    pl.semaphore_wait(barrier, expected)
    send_y(0)
    send_y(1)
    project(1)
    send_y(2)
    send_y(3)
    make_weights()
    w_copy.start()
    for t in range(CHUNKS + 3):
        if t < CHUNKS:
            stage_y(t)
        if 0 <= t - 1 < CHUNKS:
            stage_z(t - 1)
        if 0 <= t - 2 < CHUNKS:
            stage_relay(t - 2)
        if 0 <= t - 3 < CHUNKS:
            stage_response(t - 3)
    for j in range(2):
        send_tiles(j)
    for j in range(2):
        stage_x(j)

    for c in range(CHUNKS):
        for d in range(1, 4):
            y_copy(c, d).wait_send()
            z_copy(c, d).wait_send()
            m_copy(c, d).wait_send()
            n_copy(c, d).wait_send()

        @pl.when(jnp.logical_not(own_n))
        def _():
            n_copy(c, 0).wait_send()

        relay(c).wait_send()
    w_copy.wait_send()
    for j in range(2):
        for d in range(1, 4):
            x_copy(j, d).wait_send()

    @pl.when(jnp.logical_not(own_c))
    def _():
        f_arrival(0).wait_recv()

    f_arrival(1).wait_recv()
    total = frecv[0].astype(F32) + frecv[1].astype(F32)
    out_ref[:, :32, :] = total[:, :, :64]
    out_ref[:, 32:, :] = total[:, :, 64:]
    for j in range(2):
        mine = jnp.logical_and(own_c, y_lo == j)

        @pl.when(jnp.logical_not(mine))
        def _():
            f_copy(j).wait_send()


def per_device(
    pair_products, basis, val_energy, cond_energy, frequencies, valence_index, conduction_index
):
    pairs_total = pair_products.shape[1] * lax.axis_size("pair")
    vmem = pl.BlockSpec(memory_space=pltpu.VMEM)
    hbm = pl.BlockSpec(memory_space=pl.ANY)
    dma = pltpu.SemaphoreType.DMA
    return pl.pallas_call(
        functools.partial(kernel, pairs_total),
        out_shape=jax.ShapeDtypeStruct((8, 64, 64), F32),
        in_specs=[hbm] * 7,
        out_specs=vmem,
        scratch_shapes=[
            pltpu.VMEM((1, 128), F32),
            pltpu.VMEM((1, 128), F32),
            pltpu.SMEM((8,), F32),
            pltpu.VMEM((1, 512), jnp.int32),
            pltpu.VMEM((1, 512), jnp.int32),
            dma((5,)),
            pltpu.VMEM((4, 2048, 256), BF16),
            pltpu.VMEM((HALVES, 2048, 256), BF16),
            pltpu.VMEM((CHUNKS, 4, 4, 64, 128), BF16),
            pltpu.VMEM((CHUNKS, 3, 4, 64, 128), BF16),
            pltpu.VMEM((CHUNKS, 4, 64, 128), BF16),
            pltpu.VMEM((CHUNKS, 3, 64, 128), BF16),
            pltpu.VMEM((CHUNKS, 2, 4, 64, 128), BF16),
            pltpu.VMEM((CHUNKS, 2, 2, 64, 128), BF16),
            pltpu.VMEM((2, CHUNKS, 8, 128), F32),
            pltpu.VMEM((2, 512, 256), F32),
            pltpu.VMEM((2, 4, 8, 32, 128), BF16),
            pltpu.VMEM((2, 3, 8, 32, 128), BF16),
            pltpu.VMEM((2, 8, 32, 128), BF16),
            pltpu.VMEM((2, 8, 32, 128), BF16),
            dma((4,)),
            dma((HALVES,)),
            dma((CHUNKS, 3)),
            dma((CHUNKS, 3)),
            dma((CHUNKS, 3)),
            dma((CHUNKS, 3)),
            dma((CHUNKS, 3)),
            dma((CHUNKS, 3)),
            dma((CHUNKS, 4)),
            dma((CHUNKS, 4)),
            dma((CHUNKS,)),
            dma((CHUNKS,)),
            dma(()),
            dma(()),
            dma((2, 3)),
            dma((2, 3)),
            dma((2,)),
            dma((2,)),
        ],
        compiler_params=pltpu.CompilerParams(
            collective_id=0, has_side_effects=True, vmem_limit_bytes=60 * 2**20
        ),
    )(
        pair_products,
        basis,
        val_energy.reshape(1, -1),
        cond_energy.reshape(1, -1),
        frequencies,
        valence_index.reshape(1, -1),
        conduction_index.reshape(1, -1),
    )


def solution(mesh):
    placed = (P("pw", "pair"), P("pw", None), P(), P(), P(), P("pair"), P("pair"))
    return jax.shard_map(
        per_device, mesh=mesh, in_specs=placed, out_specs=P(None, "pw", "pair"), check_vma=False
    )
```

```python
import functools

import jax
import jax.numpy as jnp
from jax import lax
from jax.experimental import pallas as pl
from jax.experimental.pallas import tpu as pltpu
from jax.sharding import PartitionSpec as P

F32 = jnp.float32
BF16 = jnp.bfloat16
MESH = pl.DeviceIdType.MESH
CHUNKS = 4
HALVES = 2


def kernel(
    pairs_total,
    pp_hbm,
    basis_hbm,
    val_hbm,
    cond_hbm,
    freq_hbm,
    vidx_hbm,
    cidx_hbm,
    out_ref,
    val_ref,
    cond_ref,
    freq_ref,
    vidx_ref,
    cidx_ref,
    small_sem,
    basis_v,
    pp_v,
    psend,
    yrecv,
    zsend,
    zrecv,
    own_rows,
    mbuf,
    nbuf,
    wbuf,
    acc,
    fsend,
    frecv,
    basis_sem,
    pp_sem,
    y_ss,
    y_rs,
    z_ss,
    z_rs,
    m_ss,
    m_rs,
    n_ss,
    n_rs,
    nx_ss,
    nx_rs,
    r_ss,
    r_rs,
    w_ss,
    w_rs,
    wx_ss,
    wx_rs,
    f_ss,
    f_rs,
):
    pair, pw = lax.axis_index("pair"), lax.axis_index("pw")
    x, zl, cc = pair // 4, (pair // 2) % 2, pair % 2
    zh, y = pw // 4, pw % 4
    y_hi, y_lo = y // 2, y % 2

    def dev(x=x, zl=zl, cc=cc, zh=zh, y=y):
        return {"pair": x * 4 + zl * 2 + cc, "pw": zh * 4 + y}

    def basis_load(zb):
        return pltpu.make_async_copy(
            basis_hbm.at[:, pl.ds(pl.multiple_of(zb * 256, 256), 256)],
            basis_v.at[zb],
            basis_sem.at[zb],
        )

    def pp_load(h):
        return pltpu.make_async_copy(
            pp_hbm.at[:, pl.ds(h * 256, 256)], pp_v.at[h], pp_sem.at[h]
        )

    pp_load(0).start()
    for zb in range(4):
        basis_load(zb).start()
    pp_load(1).start()
    small_loads = [
        pltpu.make_async_copy(source, target, small_sem.at[i])
        for i, (source, target) in enumerate(
            [
                (val_hbm, val_ref),
                (cond_hbm, cond_ref),
                (freq_hbm, freq_ref),
                (vidx_hbm, vidx_ref),
                (cidx_hbm, cidx_ref),
            ]
        )
    ]
    for load in small_loads:
        load.start()

    own_n = y_hi == cc
    own_m = x == zh
    own_c = jnp.logical_and(y == 2 * zl + cc, y_hi == cc)
    barrier = pltpu.get_barrier_semaphore()

    def greet(device):
        pl.semaphore_signal(barrier, inc=1, device_id=device, device_id_type=MESH)

    for d in range(1, 4):
        greet(dev(y=(y + 4 - d) % 4))
        greet(dev(zh=(zh + 4 - d) % 4))
        greet(dev(x=(x + 4 - d) % 4))
    greet(dev(cc=1 - cc))
    for e in range(4):
        source = dev(x=(x + e) % 4, zh=x)
        if e == 0:

            @pl.when(jnp.logical_not(own_m))
            def _():
                greet(source)
        else:
            greet(source)
    for j in range(2):
        for pc in range(2):
            mine = jnp.logical_and(own_n, jnp.logical_and(y_lo == j, cc == pc))

            @pl.when(jnp.logical_not(mine))
            def _():
                greet(dev(y=2 * cc + j, cc=pc))

    greet(dev(zl=1 - zl, y=2 * zl + cc, cc=y_hi))

    @pl.when(jnp.logical_not(own_c))
    def _():
        greet(dev(y=2 * zl + cc, cc=y_hi))

    expected = 20 - jnp.where(own_m, 1, 0) - jnp.where(own_n, 1, 0) - jnp.where(own_c, 1, 0)

    def y_copy(c, d):
        return pltpu.make_async_remote_copy(
            src_ref=psend.at[c, (y + d) % 4],
            dst_ref=yrecv.at[c, d - 1],
            send_sem=y_ss.at[c, d - 1],
            recv_sem=y_rs.at[c, d - 1],
            device_id=dev(y=(y + d) % 4),
            device_id_type=MESH,
        )

    def y_part(c, d, zb):
        return pltpu.make_async_remote_copy(
            src_ref=psend.at[c, (y + d) % 4, zb],
            dst_ref=yrecv.at[c, d - 1, zb],
            send_sem=y_ss.at[c, d - 1],
            recv_sem=y_rs.at[c, d - 1],
            device_id=dev(y=(y + d) % 4),
            device_id_type=MESH,
        )

    def z_copy(c, d):
        return pltpu.make_async_remote_copy(
            src_ref=zsend.at[c, (zh + d) % 4],
            dst_ref=zrecv.at[c, d - 1],
            send_sem=z_ss.at[c, d - 1],
            recv_sem=z_rs.at[c, d - 1],
            device_id=dev(zh=(zh + d) % 4),
            device_id_type=MESH,
        )

    def m_copy(c, d):
        return pltpu.make_async_remote_copy(
            src_ref=own_rows.at[c],
            dst_ref=mbuf.at[c, cc, x],
            send_sem=m_ss.at[c, d],
            recv_sem=m_rs.at[c, x],
            device_id=dev(x=zh, zh=(zh + d) % 4),
            device_id_type=MESH,
        )

    def m_arrival(c, e):
        return pltpu.make_async_remote_copy(
            src_ref=own_rows.at[c],
            dst_ref=mbuf.at[c, cc, (x + e) % 4],
            send_sem=m_ss.at[c, 0],
            recv_sem=m_rs.at[c, (x + e) % 4],
            device_id=dev(cc=1 - cc),
            device_id_type=MESH,
        )

    def n_copy(c, d):
        return pltpu.make_async_remote_copy(
            src_ref=own_rows.at[c],
            dst_ref=nbuf.at[c, x, y_lo, cc],
            send_sem=n_ss.at[c, d],
            recv_sem=n_rs.at[c, y_lo * 2 + cc],
            device_id=dev(y=(y + d) % 4, cc=y_hi),
            device_id_type=MESH,
        )

    def n_arrival(c, j, pc):
        return pltpu.make_async_remote_copy(
            src_ref=own_rows.at[c],
            dst_ref=nbuf.at[c, x, j, pc],
            send_sem=n_ss.at[c, 0],
            recv_sem=n_rs.at[c, j * 2 + pc],
            device_id=dev(cc=1 - cc),
            device_id_type=MESH,
        )

    def nx_copy(c, d):
        return pltpu.make_async_remote_copy(
            src_ref=nbuf.at[c, x],
            dst_ref=nbuf.at[c, x],
            send_sem=nx_ss.at[c, d - 1],
            recv_sem=nx_rs.at[c, d - 1],
            device_id=dev(x=(x + d) % 4),
            device_id_type=MESH,
        )

    def relay(c):
        return pltpu.make_async_remote_copy(
            src_ref=mbuf.at[c, cc],
            dst_ref=mbuf.at[c, cc],
            send_sem=r_ss.at[c],
            recv_sem=r_rs.at[c],
            device_id=dev(cc=1 - cc),
            device_id_type=MESH,
        )

    def wx_copy(d):
        return pltpu.make_async_remote_copy(
            src_ref=wbuf.at[x],
            dst_ref=wbuf.at[x],
            send_sem=wx_ss.at[d - 1],
            recv_sem=wx_rs.at[d - 1],
            device_id=dev(x=(x + d) % 4),
            device_id_type=MESH,
        )

    w_copy = pltpu.make_async_remote_copy(
        src_ref=wbuf.at[x, cc],
        dst_ref=wbuf.at[x, cc],
        send_sem=w_ss,
        recv_sem=w_rs,
        device_id=dev(cc=1 - cc),
        device_id_type=MESH,
    )

    def f_copy(j):
        slot = (y_hi + zl) % 2
        return pltpu.make_async_remote_copy(
            src_ref=fsend.at[j],
            dst_ref=frecv.at[slot],
            send_sem=f_ss.at[j],
            recv_sem=f_rs.at[slot],
            device_id=dev(y=2 * cc + j, zl=y_hi, cc=y_lo),
            device_id_type=MESH,
        )

    def f_arrival(slot):
        return pltpu.make_async_remote_copy(
            src_ref=fsend.at[0],
            dst_ref=frecv.at[slot],
            send_sem=f_ss.at[0],
            recv_sem=f_rs.at[slot],
            device_id=dev(cc=1 - cc),
            device_id_type=MESH,
        )

    def project_rows(h, zb):
        block = lax.dot_general(
            basis_v[zb], pp_v[h], (((0,), (0,)), ((), ())), preferred_element_type=F32
        )
        block = block.astype(BF16).reshape(4, 64, 256)
        psend[2 * h, :, zb] = block[:, :, :128]
        psend[2 * h + 1, :, zb] = block[:, :, 128:]

    def send_y(c):
        for d in (2, 1, 3):
            y_copy(c, d).start()

    def send_y_part(c, zb):
        for d in (2, 1, 3):
            y_part(c, d, zb).start()

    def make_weights():
        for load in small_loads:
            load.wait()
        levels = lax.broadcasted_iota(jnp.int32, (128, 512), 0)

        def lookup(index, table):
            column = jnp.transpose(jnp.broadcast_to(table, (128, 128)))[:, :1]
            return jnp.sum(jnp.where(levels == index, column, 0.0), axis=0, keepdims=True)

        gap = lookup(cidx_ref[...], cond_ref[...]) - lookup(vidx_ref[...], val_ref[...])
        for k in range(8):
            freq = freq_ref[k]
            weight = -4.0 * gap / (gap * gap + freq * freq) / pairs_total
            for c in range(CHUNKS):
                wbuf[x, cc, c, k : k + 1, :] = weight[:, c * 128 : (c + 1) * 128]

    def stage_y(c):
        for d in range(1, 4):
            y_copy(c, d).wait_recv()
        total = psend[c, y].astype(F32)
        for d in range(3):
            total += yrecv[c, d].astype(F32)
        zsend[c] = total.astype(BF16)
        for d in (2, 1, 3):
            z_copy(c, d).start()

    def stage_z(c):
        for d in range(1, 4):
            z_copy(c, d).wait_recv()
        total = zsend[c, zh].astype(F32)
        for d in range(3):
            total += zrecv[c, d].astype(F32)
        own = total.astype(BF16)
        own_rows[c] = own

        @pl.when(own_m)
        def _():
            mbuf[c, cc, x] = own

        @pl.when(own_n)
        def _():
            nbuf[c, x, y_lo, cc] = own

        for d in (2, 1, 3):
            n_copy(c, d).start()

        @pl.when(jnp.logical_not(own_n))
        def _():
            n_copy(c, 0).start()

        for d in (2, 1, 3):
            m_copy(c, d).start()

        @pl.when(jnp.logical_not(own_m))
        def _():
            m_copy(c, 0).start()

    def stage_relay(c):
        for j in range(2):
            for pc in range(2):
                mine = jnp.logical_and(own_n, jnp.logical_and(y_lo == j, cc == pc))

                @pl.when(jnp.logical_not(mine))
                def _():
                    n_arrival(c, j, pc).wait_recv()

        for d in (2, 1, 3):
            nx_copy(c, d).start()

        @pl.when(jnp.logical_not(own_m))
        def _():
            m_arrival(c, 0).wait_recv()

        for e in range(1, 4):
            m_arrival(c, e).wait_recv()
        relay(c).start()

    def stage_response(c):
        if c == 0:
            for d in range(1, 4):
                wx_copy(d).wait_recv()
        relay(c).wait_recv()
        groups = [(xs, pc) for xs in range(4) for pc in range(2)]
        left = jnp.concatenate(
            [
                (wbuf[xs, pc, c][:, None, :] * mbuf[c, pc, xs].astype(F32)[None])
                .astype(BF16)
                .reshape(512, 128)
                for xs, pc in groups
            ],
            axis=1,
        )
        for d in range(1, 4):
            nx_copy(c, d).wait_recv()
        right = jnp.concatenate(
            [nbuf[c, xs, :, pc].reshape(128, 128) for xs, pc in groups], axis=1
        )
        part = lax.dot_general(left, right, (((1,), (1,)), ((), ())), preferred_element_type=F32)
        if c == 0:
            acc[...] = part
        else:
            acc[...] += part

    def send_tile(j):
        rows = acc[...].reshape(8, 64, 128)[:, :, j * 64 : (j + 1) * 64]
        tile = jnp.concatenate([rows[:, :32], rows[:, 32:]], axis=2).astype(BF16)
        fsend[j] = tile
        mine = jnp.logical_and(own_c, y_lo == j)

        @pl.when(mine)
        def _():
            frecv[0] = tile

        @pl.when(jnp.logical_not(mine))
        def _():
            f_copy(j).start()

    pp_load(0).wait()
    basis_load(0).wait()
    project_rows(0, 0)
    pl.semaphore_wait(barrier, expected)
    send_y_part(0, 0)

    def first_rows(zb, carry):
        basis_load(zb).wait()
        project_rows(0, zb)
        send_y_part(0, zb)
        return carry

    lax.fori_loop(1, 4, first_rows, 0)
    send_y(1)
    pp_load(1).wait()

    def second_rows(zb, carry):
        project_rows(1, zb)
        return carry

    lax.fori_loop(0, 4, second_rows, 0)
    send_y(2)
    send_y(3)
    make_weights()
    w_copy.start()
    w_copy.wait_recv()
    for d in range(1, 4):
        wx_copy(d).start()
    for t in range(CHUNKS + 3):
        if t < CHUNKS:
            stage_y(t)
        if 0 <= t - 1 < CHUNKS:
            stage_z(t - 1)
        if 0 <= t - 2 < CHUNKS:
            stage_relay(t - 2)
        if 0 <= t - 3 < CHUNKS:
            stage_response(t - 3)
    for j in range(2):
        send_tile(j)

    for c in range(CHUNKS):
        for d in range(1, 4):
            y_copy(c, d).wait_send()
            z_copy(c, d).wait_send()
            m_copy(c, d).wait_send()
            n_copy(c, d).wait_send()
            nx_copy(c, d).wait_send()

        @pl.when(jnp.logical_not(own_n))
        def _():
            n_copy(c, 0).wait_send()

        @pl.when(jnp.logical_not(own_m))
        def _():
            m_copy(c, 0).wait_send()

        relay(c).wait_send()
    w_copy.wait_send()
    for d in range(1, 4):
        wx_copy(d).wait_send()

    @pl.when(jnp.logical_not(own_c))
    def _():
        f_arrival(0).wait_recv()

    f_arrival(1).wait_recv()
    total = frecv[0].astype(F32) + frecv[1].astype(F32)
    rows = jnp.concatenate([total[:, :, :64], total[:, :, 64:]], axis=1)
    out_ref[...] = jnp.swapaxes(rows, 1, 2)
    for j in range(2):
        mine = jnp.logical_and(own_c, y_lo == j)

        @pl.when(jnp.logical_not(mine))
        def _():
            f_copy(j).wait_send()


def per_device(
    pair_products, basis, val_energy, cond_energy, frequencies, valence_index, conduction_index
):
    pairs_total = pair_products.shape[1] * lax.axis_size("pair")
    vmem = pl.BlockSpec(memory_space=pltpu.VMEM)
    hbm = pl.BlockSpec(memory_space=pl.ANY)
    dma = pltpu.SemaphoreType.DMA
    return pl.pallas_call(
        functools.partial(kernel, pairs_total),
        out_shape=jax.ShapeDtypeStruct((8, 64, 64), F32),
        in_specs=[hbm] * 7,
        out_specs=vmem,
        scratch_shapes=[
            pltpu.VMEM((1, 128), F32),
            pltpu.VMEM((1, 128), F32),
            pltpu.SMEM((8,), F32),
            pltpu.VMEM((1, 512), jnp.int32),
            pltpu.VMEM((1, 512), jnp.int32),
            dma((5,)),
            pltpu.VMEM((4, 2048, 256), BF16),
            pltpu.VMEM((HALVES, 2048, 256), BF16),
            pltpu.VMEM((CHUNKS, 4, 4, 64, 128), BF16),
            pltpu.VMEM((CHUNKS, 3, 4, 64, 128), BF16),
            pltpu.VMEM((CHUNKS, 4, 64, 128), BF16),
            pltpu.VMEM((CHUNKS, 3, 64, 128), BF16),
            pltpu.VMEM((CHUNKS, 64, 128), BF16),
            pltpu.VMEM((CHUNKS, 2, 4, 64, 128), BF16),
            pltpu.VMEM((CHUNKS, 4, 2, 2, 64, 128), BF16),
            pltpu.VMEM((4, 2, CHUNKS, 8, 128), F32),
            pltpu.VMEM((512, 128), F32),
            pltpu.VMEM((2, 8, 32, 128), BF16),
            pltpu.VMEM((2, 8, 32, 128), BF16),
            dma((4,)),
            dma((HALVES,)),
            dma((CHUNKS, 3)),
            dma((CHUNKS, 3)),
            dma((CHUNKS, 3)),
            dma((CHUNKS, 3)),
            dma((CHUNKS, 4)),
            dma((CHUNKS, 4)),
            dma((CHUNKS, 4)),
            dma((CHUNKS, 4)),
            dma((CHUNKS, 3)),
            dma((CHUNKS, 3)),
            dma((CHUNKS,)),
            dma((CHUNKS,)),
            dma(()),
            dma(()),
            dma((3,)),
            dma((3,)),
            dma((2,)),
            dma((2,)),
        ],
        compiler_params=pltpu.CompilerParams(
            collective_id=0, has_side_effects=True, vmem_limit_bytes=56 * 2**20
        ),
    )(
        pair_products,
        basis,
        val_energy.reshape(1, -1),
        cond_energy.reshape(1, -1),
        frequencies,
        valence_index.reshape(1, -1),
        conduction_index.reshape(1, -1),
    )


def solution(mesh):
    placed = (P("pw", "pair"), P("pw", None), P(), P(), P(), P("pair"), P("pair"))
    return jax.shard_map(
        per_device, mesh=mesh, in_specs=placed, out_specs=P(None, "pw", "pair"), check_vma=False
    )
```

```python
import functools

import jax
import jax.numpy as jnp
from jax import lax
from jax.experimental import pallas as pl
from jax.experimental.pallas import tpu as pltpu
from jax.sharding import PartitionSpec as P

F32 = jnp.float32
BF16 = jnp.bfloat16
MESH = pl.DeviceIdType.MESH
CHUNKS = 4
HALVES = 2
LAST = CHUNKS - 1


def kernel(
    pairs_total,
    pp_hbm,
    basis_hbm,
    val_hbm,
    cond_hbm,
    freq_hbm,
    vidx_hbm,
    cidx_hbm,
    out_ref,
    val_ref,
    cond_ref,
    freq_ref,
    vidx_ref,
    cidx_ref,
    small_sem,
    basis_v,
    pp_v,
    psend,
    passing,
    passed_on,
    yrecv,
    zsend,
    zrecv,
    own_rows,
    mbuf,
    nbuf,
    wbuf,
    acc,
    fsend,
    frecv,
    basis_sem,
    pp_sem,
    y_ss,
    y_rs,
    z_ss,
    z_rs,
    m_ss,
    m_rs,
    n_ss,
    n_rs,
    last_ss,
    last_rs,
    nx_ss,
    nx_rs,
    r_ss,
    r_rs,
    w_ss,
    w_rs,
    wx_ss,
    wx_rs,
    f_ss,
    f_rs,
):
    pair, pw = lax.axis_index("pair"), lax.axis_index("pw")
    x, zl, cc = pair // 4, (pair // 2) % 2, pair % 2
    zh, y = pw // 4, pw % 4
    y_hi, y_lo = y // 2, y % 2

    def dev(x=x, zl=zl, cc=cc, zh=zh, y=y):
        return {"pair": x * 4 + zl * 2 + cc, "pw": zh * 4 + y}

    def basis_load(zb):
        return pltpu.make_async_copy(
            basis_hbm.at[:, pl.ds(pl.multiple_of(zb * 256, 256), 256)],
            basis_v.at[zb],
            basis_sem.at[zb],
        )

    def pp_load(h):
        return pltpu.make_async_copy(
            pp_hbm.at[:, pl.ds(h * 256, 256)], pp_v.at[h], pp_sem.at[h]
        )

    pp_load(0).start()
    for zb in range(4):
        basis_load(zb).start()
    pp_load(1).start()
    small_loads = [
        pltpu.make_async_copy(source, target, small_sem.at[i])
        for i, (source, target) in enumerate(
            [
                (val_hbm, val_ref),
                (cond_hbm, cond_ref),
                (freq_hbm, freq_ref),
                (vidx_hbm, vidx_ref),
                (cidx_hbm, cidx_ref),
            ]
        )
    ]
    for load in small_loads:
        load.start()

    own_n = y_hi == cc
    own_m = x == zh
    own_c = jnp.logical_and(y == 2 * zl + cc, y_hi == cc)
    barrier = pltpu.get_barrier_semaphore()

    def greet(device):
        pl.semaphore_signal(barrier, inc=1, device_id=device, device_id_type=MESH)

    for d in range(1, 4):
        greet(dev(y=(y + 4 - d) % 4))
        greet(dev(zh=(zh + 4 - d) % 4))
        greet(dev(x=(x + 4 - d) % 4))
    greet(dev(cc=1 - cc))
    for e in range(4):
        source = dev(x=(x + e) % 4, zh=x)
        if e == 0:

            @pl.when(jnp.logical_not(own_m))
            def _():
                greet(source)
        else:
            greet(source)
    for j in range(2):
        for pc in range(2):
            mine = jnp.logical_and(own_n, jnp.logical_and(y_lo == j, cc == pc))
            for e in range(4):
                source = dev(x=(x + e) % 4, y=2 * cc + j, cc=pc)
                if e == 0:

                    @pl.when(jnp.logical_not(mine))
                    def _():
                        greet(source)
                else:
                    greet(source)

    greet(dev(zl=1 - zl, y=2 * zl + cc, cc=y_hi))

    @pl.when(jnp.logical_not(own_c))
    def _():
        greet(dev(y=2 * zl + cc, cc=y_hi))

    expected = 32 - jnp.where(own_m, 1, 0) - jnp.where(own_n, 1, 0) - jnp.where(own_c, 1, 0)

    def to_y(source, target, c, i, step):
        return pltpu.make_async_remote_copy(
            src_ref=source,
            dst_ref=target,
            send_sem=y_ss.at[c, i],
            recv_sem=y_rs.at[c, i],
            device_id=dev(y=(y + step) % 4),
            device_id_type=MESH,
        )

    def y_copies(c):
        if c == LAST:
            return [
                functools.partial(to_y, psend.at[c, (y + d) % 4], yrecv.at[c, d - 1], c, d - 1, d)
                for d in (2, 1, 3)
            ]
        low, high = pl.ds(0, 2), pl.ds(2, 2)
        return [
            functools.partial(to_y, psend.at[c, (y + 2) % 4, low], passing.at[c, 0], c, 0, 1),
            functools.partial(to_y, psend.at[c, (y + 3) % 4, low], yrecv.at[c, 1, low], c, 3, 3),
            functools.partial(to_y, psend.at[c, (y + 2) % 4, high], passing.at[c, 1], c, 1, 3),
            functools.partial(to_y, psend.at[c, (y + 1) % 4, high], yrecv.at[c, 0, high], c, 2, 1),
            functools.partial(to_y, passed_on.at[c, 0], yrecv.at[c, 0, low], c, 4, 1),
            functools.partial(to_y, passed_on.at[c, 1], yrecv.at[c, 1, high], c, 5, 3),
        ]

    def z_copy(c, d):
        return pltpu.make_async_remote_copy(
            src_ref=zsend.at[c, (zh + d) % 4],
            dst_ref=zrecv.at[c, d - 1],
            send_sem=z_ss.at[c, d - 1],
            recv_sem=z_rs.at[c, d - 1],
            device_id=dev(zh=(zh + d) % 4),
            device_id_type=MESH,
        )

    def m_copy(c, d):
        return pltpu.make_async_remote_copy(
            src_ref=own_rows.at[c],
            dst_ref=mbuf.at[c, cc, x],
            send_sem=m_ss.at[c, d],
            recv_sem=m_rs.at[c, x],
            device_id=dev(x=zh, zh=(zh + d) % 4),
            device_id_type=MESH,
        )

    def m_arrival(c, e):
        return pltpu.make_async_remote_copy(
            src_ref=own_rows.at[c],
            dst_ref=mbuf.at[c, cc, (x + e) % 4],
            send_sem=m_ss.at[c, 0],
            recv_sem=m_rs.at[c, (x + e) % 4],
            device_id=dev(cc=1 - cc),
            device_id_type=MESH,
        )

    def n_copy(c, d):
        return pltpu.make_async_remote_copy(
            src_ref=own_rows.at[c],
            dst_ref=nbuf.at[c, x, y_lo, cc],
            send_sem=n_ss.at[c, d],
            recv_sem=n_rs.at[c, y_lo * 2 + cc],
            device_id=dev(y=(y + d) % 4, cc=y_hi),
            device_id_type=MESH,
        )

    def n_arrival(c, j, pc):
        return pltpu.make_async_remote_copy(
            src_ref=own_rows.at[c],
            dst_ref=nbuf.at[c, x, j, pc],
            send_sem=n_ss.at[c, 0],
            recv_sem=n_rs.at[c, j * 2 + pc],
            device_id=dev(cc=1 - cc),
            device_id_type=MESH,
        )

    def last_copy(dx, dy):
        return pltpu.make_async_remote_copy(
            src_ref=own_rows.at[LAST],
            dst_ref=nbuf.at[LAST, x, y_lo, cc],
            send_sem=last_ss.at[dx, dy],
            recv_sem=last_rs.at[x, y_lo * 2 + cc],
            device_id=dev(x=(x + dx) % 4, y=(y + dy) % 4, cc=y_hi),
            device_id_type=MESH,
        )

    def last_arrival(e, j, pc):
        return pltpu.make_async_remote_copy(
            src_ref=own_rows.at[LAST],
            dst_ref=nbuf.at[LAST, (x + e) % 4, j, pc],
            send_sem=last_ss.at[0, 0],
            recv_sem=last_rs.at[(x + e) % 4, j * 2 + pc],
            device_id=dev(cc=1 - cc),
            device_id_type=MESH,
        )

    def nx_copy(c, d):
        return pltpu.make_async_remote_copy(
            src_ref=nbuf.at[c, x],
            dst_ref=nbuf.at[c, x],
            send_sem=nx_ss.at[c, d - 1],
            recv_sem=nx_rs.at[c, d - 1],
            device_id=dev(x=(x + d) % 4),
            device_id_type=MESH,
        )

    def relay(c):
        return pltpu.make_async_remote_copy(
            src_ref=mbuf.at[c, cc],
            dst_ref=mbuf.at[c, cc],
            send_sem=r_ss.at[c],
            recv_sem=r_rs.at[c],
            device_id=dev(cc=1 - cc),
            device_id_type=MESH,
        )

    def wx_copy(d):
        return pltpu.make_async_remote_copy(
            src_ref=wbuf.at[x],
            dst_ref=wbuf.at[x],
            send_sem=wx_ss.at[d - 1],
            recv_sem=wx_rs.at[d - 1],
            device_id=dev(x=(x + d) % 4),
            device_id_type=MESH,
        )

    w_copy = pltpu.make_async_remote_copy(
        src_ref=wbuf.at[x, cc],
        dst_ref=wbuf.at[x, cc],
        send_sem=w_ss,
        recv_sem=w_rs,
        device_id=dev(cc=1 - cc),
        device_id_type=MESH,
    )

    def f_copy(j):
        slot = (y_hi + zl) % 2
        return pltpu.make_async_remote_copy(
            src_ref=fsend.at[j],
            dst_ref=frecv.at[slot],
            send_sem=f_ss.at[j],
            recv_sem=f_rs.at[slot],
            device_id=dev(y=2 * cc + j, zl=y_hi, cc=y_lo),
            device_id_type=MESH,
        )

    def f_arrival(slot):
        return pltpu.make_async_remote_copy(
            src_ref=fsend.at[0],
            dst_ref=frecv.at[slot],
            send_sem=f_ss.at[0],
            recv_sem=f_rs.at[slot],
            device_id=dev(cc=1 - cc),
            device_id_type=MESH,
        )

    def project_rows(h, zb):
        block = lax.dot_general(
            basis_v[zb], pp_v[h], (((0,), (0,)), ((), ())), preferred_element_type=F32
        )
        block = block.astype(BF16).reshape(4, 64, 256)
        psend[2 * h, :, zb] = block[:, :, :128]
        psend[2 * h + 1, :, zb] = block[:, :, 128:]

    def send_y(c, begin=0, end=4):
        for copy in y_copies(c)[begin:end]:
            copy().start()

    def make_weights():
        for load in small_loads:
            load.wait()
        levels = lax.broadcasted_iota(jnp.int32, (128, 512), 0)

        def lookup(index, table):
            column = jnp.transpose(jnp.broadcast_to(table, (128, 128)))[:, :1]
            return jnp.sum(jnp.where(levels == index, column, 0.0), axis=0, keepdims=True)

        gap = lookup(cidx_ref[...], cond_ref[...]) - lookup(vidx_ref[...], val_ref[...])
        for k in range(8):
            freq = freq_ref[k]
            weight = -4.0 * gap / (gap * gap + freq * freq) / pairs_total
            for c in range(CHUNKS):
                wbuf[x, cc, c, k : k + 1, :] = weight[:, c * 128 : (c + 1) * 128]

    def stage_pass(c):
        up, _, down, _, up_next, down_next = y_copies(c)
        low, high = pl.ds(0, 2), pl.ds(2, 2)
        up().wait_recv()
        total = passing[c, 0].astype(F32) + psend[c, (y + 1) % 4, low].astype(F32)
        passed_on[c, 0] = total.astype(BF16)
        up_next().start()
        down().wait_recv()
        total = passing[c, 1].astype(F32) + psend[c, (y + 3) % 4, high].astype(F32)
        passed_on[c, 1] = total.astype(BF16)
        down_next().start()

    def stage_y(c):
        copies = y_copies(c)
        for i in (0, 1, 2) if c == LAST else (1, 3, 4, 5):
            copies[i]().wait_recv()
        total = psend[c, y].astype(F32)
        for d in range(3 if c == LAST else 2):
            total += yrecv[c, d].astype(F32)
        zsend[c] = total.astype(BF16)
        for d in (2, 1, 3):
            z_copy(c, d).start()

    def stage_z(c):
        for d in range(1, 4):
            z_copy(c, d).wait_recv()
        total = zsend[c, zh].astype(F32)
        for d in range(3):
            total += zrecv[c, d].astype(F32)
        own = total.astype(BF16)
        own_rows[c] = own

        @pl.when(own_m)
        def _():
            mbuf[c, cc, x] = own

        @pl.when(own_n)
        def _():
            nbuf[c, x, y_lo, cc] = own

        if c == LAST:
            for d in (2, 1, 3):
                m_copy(c, d).start()
            for dx in (2, 1, 3, 0):
                for dy in (2, 1, 3):
                    last_copy(dx, dy).start()
                if dx:
                    last_copy(dx, 0).start()

            @pl.when(jnp.logical_not(own_n))
            def _():
                last_copy(0, 0).start()
        else:
            for d in (2, 1, 3):
                n_copy(c, d).start()

            @pl.when(jnp.logical_not(own_n))
            def _():
                n_copy(c, 0).start()

            for d in (2, 1, 3):
                m_copy(c, d).start()

        @pl.when(jnp.logical_not(own_m))
        def _():
            m_copy(c, 0).start()

    def stage_relay(c):
        if c < LAST:
            for j in range(2):
                for pc in range(2):
                    mine = jnp.logical_and(own_n, jnp.logical_and(y_lo == j, cc == pc))

                    @pl.when(jnp.logical_not(mine))
                    def _():
                        n_arrival(c, j, pc).wait_recv()

            for d in (2, 1, 3):
                nx_copy(c, d).start()

        @pl.when(jnp.logical_not(own_m))
        def _():
            m_arrival(c, 0).wait_recv()

        for e in range(1, 4):
            m_arrival(c, e).wait_recv()
        relay(c).start()

    def stage_response(c):
        if c == 0:
            for d in range(1, 4):
                wx_copy(d).wait_recv()
        relay(c).wait_recv()
        groups = [(xs, pc) for xs in range(4) for pc in range(2)]
        left = jnp.concatenate(
            [
                (wbuf[xs, pc, c][:, None, :] * mbuf[c, pc, xs].astype(F32)[None])
                .astype(BF16)
                .reshape(512, 128)
                for xs, pc in groups
            ],
            axis=1,
        )
        if c < LAST:
            for d in range(1, 4):
                nx_copy(c, d).wait_recv()
        else:
            for j in range(2):
                for pc in range(2):
                    mine = jnp.logical_and(own_n, jnp.logical_and(y_lo == j, cc == pc))

                    @pl.when(jnp.logical_not(mine))
                    def _():
                        last_arrival(0, j, pc).wait_recv()

                    for e in range(1, 4):
                        last_arrival(e, j, pc).wait_recv()
        right = jnp.concatenate(
            [nbuf[c, xs, :, pc].reshape(128, 128) for xs, pc in groups], axis=1
        )
        part = lax.dot_general(left, right, (((1,), (1,)), ((), ())), preferred_element_type=F32)
        if c == 0:
            acc[...] = part
        else:
            acc[...] += part

    def send_tile(j):
        rows = acc[...].reshape(8, 64, 128)[:, :, j * 64 : (j + 1) * 64]
        tile = jnp.concatenate([rows[:, :32], rows[:, 32:]], axis=2).astype(BF16)
        fsend[j] = tile
        mine = jnp.logical_and(own_c, y_lo == j)

        @pl.when(mine)
        def _():
            frecv[0] = tile

        @pl.when(jnp.logical_not(mine))
        def _():
            f_copy(j).start()

    pp_load(0).wait()
    for zb in range(2):
        basis_load(zb).wait()
        project_rows(0, zb)
    pl.semaphore_wait(barrier, expected)
    send_y(0, 0, 2)
    for zb in range(2, 4):
        basis_load(zb).wait()
        project_rows(0, zb)
    send_y(0, 2, 4)
    send_y(1)
    pp_load(1).wait()

    def second_rows(zb, carry):
        project_rows(1, zb)
        return carry

    lax.fori_loop(0, 4, second_rows, 0)
    stage_pass(0)
    send_y(2)
    stage_pass(1)
    send_y(3)
    make_weights()
    w_copy.start()
    stage_y(0)
    stage_pass(2)
    w_copy.wait_recv()
    for d in range(1, 4):
        wx_copy(d).start()
    for t in range(1, CHUNKS + 3):
        if t < CHUNKS:
            stage_y(t)
        if 0 <= t - 1 < CHUNKS:
            stage_z(t - 1)
        if 0 <= t - 2 < CHUNKS:
            stage_relay(t - 2)
        if 0 <= t - 3 < CHUNKS:
            stage_response(t - 3)
    for j in range(2):
        send_tile(j)

    for c in range(CHUNKS):
        for copy in y_copies(c):
            copy().wait_send()
        for d in range(1, 4):
            z_copy(c, d).wait_send()
            m_copy(c, d).wait_send()
            if c < LAST:
                n_copy(c, d).wait_send()
                nx_copy(c, d).wait_send()

        @pl.when(jnp.logical_not(own_n))
        def _():
            if c < LAST:
                n_copy(c, 0).wait_send()
            else:
                last_copy(0, 0).wait_send()

        @pl.when(jnp.logical_not(own_m))
        def _():
            m_copy(c, 0).wait_send()

        relay(c).wait_send()
    w_copy.wait_send()
    for dx in range(4):
        for dy in range(4):
            if dx or dy:
                last_copy(dx, dy).wait_send()
    for d in range(1, 4):
        wx_copy(d).wait_send()

    @pl.when(jnp.logical_not(own_c))
    def _():
        f_arrival(0).wait_recv()

    f_arrival(1).wait_recv()
    total = frecv[0].astype(F32) + frecv[1].astype(F32)
    rows = jnp.concatenate([total[:, :, :64], total[:, :, 64:]], axis=1)
    out_ref[...] = jnp.swapaxes(rows, 1, 2)
    for j in range(2):
        mine = jnp.logical_and(own_c, y_lo == j)

        @pl.when(jnp.logical_not(mine))
        def _():
            f_copy(j).wait_send()


def per_device(
    pair_products, basis, val_energy, cond_energy, frequencies, valence_index, conduction_index
):
    pairs_total = pair_products.shape[1] * lax.axis_size("pair")
    vmem = pl.BlockSpec(memory_space=pltpu.VMEM)
    hbm = pl.BlockSpec(memory_space=pl.ANY)
    dma = pltpu.SemaphoreType.DMA
    return pl.pallas_call(
        functools.partial(kernel, pairs_total),
        out_shape=jax.ShapeDtypeStruct((8, 64, 64), F32),
        in_specs=[hbm] * 7,
        out_specs=vmem,
        scratch_shapes=[
            pltpu.VMEM((1, 128), F32),
            pltpu.VMEM((1, 128), F32),
            pltpu.SMEM((8,), F32),
            pltpu.VMEM((1, 512), jnp.int32),
            pltpu.VMEM((1, 512), jnp.int32),
            dma((5,)),
            pltpu.VMEM((4, 2048, 256), BF16),
            pltpu.VMEM((HALVES, 2048, 256), BF16),
            pltpu.VMEM((CHUNKS, 4, 4, 64, 128), BF16),
            pltpu.VMEM((LAST, 2, 2, 64, 128), BF16),
            pltpu.VMEM((LAST, 2, 2, 64, 128), BF16),
            pltpu.VMEM((CHUNKS, 3, 4, 64, 128), BF16),
            pltpu.VMEM((CHUNKS, 4, 64, 128), BF16),
            pltpu.VMEM((CHUNKS, 3, 64, 128), BF16),
            pltpu.VMEM((CHUNKS, 64, 128), BF16),
            pltpu.VMEM((CHUNKS, 2, 4, 64, 128), BF16),
            pltpu.VMEM((CHUNKS, 4, 2, 2, 64, 128), BF16),
            pltpu.VMEM((4, 2, CHUNKS, 8, 128), F32),
            pltpu.VMEM((512, 128), F32),
            pltpu.VMEM((2, 8, 32, 128), BF16),
            pltpu.VMEM((2, 8, 32, 128), BF16),
            dma((4,)),
            dma((HALVES,)),
            dma((CHUNKS, 6)),
            dma((CHUNKS, 6)),
            dma((CHUNKS, 3)),
            dma((CHUNKS, 3)),
            dma((CHUNKS, 4)),
            dma((CHUNKS, 4)),
            dma((CHUNKS, 4)),
            dma((CHUNKS, 4)),
            dma((4, 4)),
            dma((4, 4)),
            dma((CHUNKS, 3)),
            dma((CHUNKS, 3)),
            dma((CHUNKS,)),
            dma((CHUNKS,)),
            dma(()),
            dma(()),
            dma((3,)),
            dma((3,)),
            dma((2,)),
            dma((2,)),
        ],
        compiler_params=pltpu.CompilerParams(
            collective_id=0, has_side_effects=True, vmem_limit_bytes=56 * 2**20
        ),
    )(
        pair_products,
        basis,
        val_energy.reshape(1, -1),
        cond_energy.reshape(1, -1),
        frequencies,
        valence_index.reshape(1, -1),
        conduction_index.reshape(1, -1),
    )


def solution(mesh):
    placed = (P("pw", "pair"), P("pw", None), P(), P(), P(), P("pair"), P("pair"))
    return jax.shard_map(
        per_device, mesh=mesh, in_specs=placed, out_specs=P(None, "pw", "pair"), check_vma=False
    )
```

```python
import functools

import jax
import jax.numpy as jnp
from jax import lax
from jax.experimental import pallas as pl
from jax.experimental.pallas import tpu as pltpu
from jax.sharding import PartitionSpec as P

F32 = jnp.float32
BF16 = jnp.bfloat16
MESH = pl.DeviceIdType.MESH
CHUNKS = 4
CROSSED = 1
HALF = 32
HALVES = 2


def kernel(
    pairs_total,
    pp_hbm,
    basis_hbm,
    val_hbm,
    cond_hbm,
    freq_hbm,
    vidx_hbm,
    cidx_hbm,
    out_ref,
    val_ref,
    cond_ref,
    freq_ref,
    vidx_ref,
    cidx_ref,
    small_sem,
    basis_v,
    pp_v,
    psend,
    yrecv,
    zsend,
    zrecv,
    crossed_z,
    crossed_y,
    crossed_mine,
    own_rows,
    mbuf,
    n_low,
    n_high,
    over_x,
    wbuf,
    acc,
    fsend,
    frecv,
    basis_sem,
    pp_sem,
    y_ss,
    y_rs,
    z_ss,
    z_rs,
    m_ss,
    m_rs,
    n_ss,
    n_rs,
    nx_ss,
    nx_rs,
    xf_ss,
    xf_rs,
    xn_ss,
    xn_rs,
    r_ss,
    r_rs,
    w_ss,
    w_rs,
    wx_ss,
    wx_rs,
    f_ss,
    f_rs,
):
    pair, pw = lax.axis_index("pair"), lax.axis_index("pw")
    x, zl, cc = pair // 4, (pair // 2) % 2, pair % 2
    zh, y = pw // 4, pw % 4
    y_hi, y_lo = y // 2, y % 2

    def dev(x=x, zl=zl, cc=cc, zh=zh, y=y):
        return {"pair": x * 4 + zl * 2 + cc, "pw": zh * 4 + y}

    def basis_load(zb):
        return pltpu.make_async_copy(
            basis_hbm.at[:, pl.ds(pl.multiple_of(zb * 256, 256), 256)],
            basis_v.at[zb],
            basis_sem.at[zb],
        )

    def pp_load(h):
        return pltpu.make_async_copy(
            pp_hbm.at[:, pl.ds(h * 256, 256)], pp_v.at[h], pp_sem.at[h]
        )

    pp_load(0).start()
    row_order = (2, 1, 3, 0)
    for d in row_order:
        basis_load((zh + d) % 4).start()
    pp_load(1).start()
    small_loads = [
        pltpu.make_async_copy(source, target, small_sem.at[i])
        for i, (source, target) in enumerate(
            [
                (val_hbm, val_ref),
                (cond_hbm, cond_ref),
                (freq_hbm, freq_ref),
                (vidx_hbm, vidx_ref),
                (cidx_hbm, cidx_ref),
            ]
        )
    ]
    for load in small_loads:
        load.start()

    own_n = y_hi == cc
    own_m = x == zh
    own_c = jnp.logical_and(y == 2 * zl + cc, y_hi == cc)
    barrier = pltpu.get_barrier_semaphore()

    def greet(device):
        pl.semaphore_signal(barrier, inc=1, device_id=device, device_id_type=MESH)

    for d in range(1, 4):
        greet(dev(y=(y + 4 - d) % 4))
        greet(dev(zh=(zh + 4 - d) % 4))
        greet(dev(x=(x + 4 - d) % 4))
    greet(dev(cc=1 - cc))
    for e in range(4):
        source = dev(x=(x + e) % 4, zh=x)
        if e == 0:

            @pl.when(jnp.logical_not(own_m))
            def _():
                greet(source)
        else:
            greet(source)
    for j in range(2):
        for pc in range(2):
            mine = jnp.logical_and(own_n, jnp.logical_and(y_lo == j, cc == pc))

            @pl.when(jnp.logical_not(mine))
            def _():
                greet(dev(y=2 * cc + j, cc=pc))

    greet(dev(zl=1 - zl, y=2 * zl + cc, cc=y_hi))

    @pl.when(jnp.logical_not(own_c))
    def _():
        greet(dev(y=2 * zl + cc, cc=y_hi))

    expected = 20 - jnp.where(own_m, 1, 0) - jnp.where(own_n, 1, 0) - jnp.where(own_c, 1, 0)

    def y_copy(c, d):
        return pltpu.make_async_remote_copy(
            src_ref=psend.at[c, (y + d) % 4],
            dst_ref=yrecv.at[c, d - 1],
            send_sem=y_ss.at[c, d - 1],
            recv_sem=y_rs.at[c, d - 1],
            device_id=dev(y=(y + d) % 4),
            device_id_type=MESH,
        )

    def y_part(c, d, zb):
        return pltpu.make_async_remote_copy(
            src_ref=psend.at[c, (y + d) % 4, zb],
            dst_ref=yrecv.at[c, d - 1, zb],
            send_sem=y_ss.at[c, d - 1],
            recv_sem=y_rs.at[c, d - 1],
            device_id=dev(y=(y + d) % 4),
            device_id_type=MESH,
        )

    def z_copy(c, d):
        return pltpu.make_async_remote_copy(
            src_ref=zsend.at[c, (zh + d) % 4],
            dst_ref=zrecv.at[c, d - 1],
            send_sem=z_ss.at[c, d - 1],
            recv_sem=z_rs.at[c, d - 1],
            device_id=dev(zh=(zh + d) % 4),
            device_id_type=MESH,
        )

    def zc_copy(d):
        return pltpu.make_async_remote_copy(
            src_ref=psend.at[CROSSED, :, (zh + d) % 4],
            dst_ref=crossed_z.at[d - 1],
            send_sem=z_ss.at[CROSSED, d - 1],
            recv_sem=z_rs.at[CROSSED, d - 1],
            device_id=dev(zh=(zh + d) % 4),
            device_id_type=MESH,
        )

    def yc_copy(d):
        return pltpu.make_async_remote_copy(
            src_ref=crossed_y.at[(y + d) % 4],
            dst_ref=crossed_mine.at[d - 1],
            send_sem=y_ss.at[CROSSED, d - 1],
            recv_sem=y_rs.at[CROSSED, d - 1],
            device_id=dev(y=(y + d) % 4),
            device_id_type=MESH,
        )

    def m_copy(c, d):
        return pltpu.make_async_remote_copy(
            src_ref=own_rows.at[c],
            dst_ref=mbuf.at[c, cc, x],
            send_sem=m_ss.at[c, d],
            recv_sem=m_rs.at[c, x],
            device_id=dev(x=zh, zh=(zh + d) % 4),
            device_id_type=MESH,
        )

    def m_arrival(c, e):
        return pltpu.make_async_remote_copy(
            src_ref=own_rows.at[c],
            dst_ref=mbuf.at[c, cc, (x + e) % 4],
            send_sem=m_ss.at[c, 0],
            recv_sem=m_rs.at[c, (x + e) % 4],
            device_id=dev(cc=1 - cc),
            device_id_type=MESH,
        )

    low, high = pl.ds(0, HALF), pl.ds(HALF, HALF)

    def remote(source, target, send_sem, recv_sem, device):
        return pltpu.make_async_remote_copy(
            src_ref=source,
            dst_ref=target,
            send_sem=send_sem,
            recv_sem=recv_sem,
            device_id=device,
            device_id_type=MESH,
        )

    sibling = dev(cc=1 - cc)

    def n_copy(c, d):
        return remote(
            own_rows.at[c, low],
            n_low.at[c, x, y_lo, cc],
            n_ss.at[c, d],
            n_rs.at[c, y_lo * 2 + cc],
            dev(y=(y + d) % 4, cc=y_hi),
        )

    def n_arrival(c, j, pc):
        return remote(
            own_rows.at[c, low],
            n_low.at[c, x, j, pc],
            n_ss.at[c, 0],
            n_rs.at[c, j * 2 + pc],
            sibling,
        )

    def nx_copy(c, d):
        return remote(
            n_low.at[c, x],
            n_low.at[c, x],
            nx_ss.at[c, d - 1],
            nx_rs.at[c, d - 1],
            dev(x=(x + d) % 4),
        )

    def xf_copy(c, d):
        return remote(
            own_rows.at[c, high],
            over_x.at[c, x],
            xf_ss.at[c, d - 1],
            xf_rs.at[c, d - 1],
            dev(x=(x + d) % 4),
        )

    def xn_copy(c, d):
        return remote(
            over_x.at[c],
            n_high.at[c, y_lo, cc],
            xn_ss.at[c, d],
            xn_rs.at[c, y_lo * 2 + cc],
            dev(y=(y + d) % 4, cc=y_hi),
        )

    def xn_arrival(c, j, pc):
        return remote(
            over_x.at[c],
            n_high.at[c, j, pc],
            xn_ss.at[c, 0],
            xn_rs.at[c, j * 2 + pc],
            sibling,
        )

    def relay(c):
        return pltpu.make_async_remote_copy(
            src_ref=mbuf.at[c, cc],
            dst_ref=mbuf.at[c, cc],
            send_sem=r_ss.at[c],
            recv_sem=r_rs.at[c],
            device_id=dev(cc=1 - cc),
            device_id_type=MESH,
        )

    def wx_copy(d):
        return pltpu.make_async_remote_copy(
            src_ref=wbuf.at[x],
            dst_ref=wbuf.at[x],
            send_sem=wx_ss.at[d - 1],
            recv_sem=wx_rs.at[d - 1],
            device_id=dev(x=(x + d) % 4),
            device_id_type=MESH,
        )

    w_copy = pltpu.make_async_remote_copy(
        src_ref=wbuf.at[x, cc],
        dst_ref=wbuf.at[x, cc],
        send_sem=w_ss,
        recv_sem=w_rs,
        device_id=dev(cc=1 - cc),
        device_id_type=MESH,
    )

    def f_copy(j):
        slot = (y_hi + zl) % 2
        return pltpu.make_async_remote_copy(
            src_ref=fsend.at[j],
            dst_ref=frecv.at[slot],
            send_sem=f_ss.at[j],
            recv_sem=f_rs.at[slot],
            device_id=dev(y=2 * cc + j, zl=y_hi, cc=y_lo),
            device_id_type=MESH,
        )

    def f_arrival(slot):
        return pltpu.make_async_remote_copy(
            src_ref=fsend.at[0],
            dst_ref=frecv.at[slot],
            send_sem=f_ss.at[0],
            recv_sem=f_rs.at[slot],
            device_id=dev(cc=1 - cc),
            device_id_type=MESH,
        )

    def project_rows(h, zb):
        block = lax.dot_general(
            basis_v[zb], pp_v[h], (((0,), (0,)), ((), ())), preferred_element_type=F32
        )
        block = block.astype(BF16).reshape(4, 64, 256)
        psend[2 * h, :, zb] = block[:, :, :128]
        psend[2 * h + 1, :, zb] = block[:, :, 128:]

    def send_y(c):
        for d in (2, 1, 3):
            y_copy(c, d).start()

    def send_y_part(c, zb):
        for d in (2, 1, 3):
            y_part(c, d, zb).start()

    def make_weights():
        for load in small_loads:
            load.wait()
        levels = lax.broadcasted_iota(jnp.int32, (128, 512), 0)

        def lookup(index, table):
            column = jnp.transpose(jnp.broadcast_to(table, (128, 128)))[:, :1]
            return jnp.sum(jnp.where(levels == index, column, 0.0), axis=0, keepdims=True)

        gap = lookup(cidx_ref[...], cond_ref[...]) - lookup(vidx_ref[...], val_ref[...])
        for k in range(8):
            freq = freq_ref[k]
            weight = -4.0 * gap / (gap * gap + freq * freq) / pairs_total
            for c in range(CHUNKS):
                wbuf[x, cc, c, k : k + 1, :] = weight[:, c * 128 : (c + 1) * 128]

    def stage_y(c):
        for d in range(1, 4):
            y_copy(c, d).wait_recv()
        total = psend[c, y].astype(F32)
        for d in range(3):
            total += yrecv[c, d].astype(F32)
        zsend[c] = total.astype(BF16)
        for d in (2, 1, 3):
            z_copy(c, d).start()

    def stage_z(c):
        for d in range(1, 4):
            z_copy(c, d).wait_recv()
        total = zsend[c, zh].astype(F32)
        for d in range(3):
            total += zrecv[c, d].astype(F32)
        share(c, total)

    def stage_crossed_z():
        for d in range(1, 4):
            zc_copy(d).wait_recv()
        total = psend[CROSSED, :, zh].astype(F32)
        for d in range(3):
            total += crossed_z[d].astype(F32)
        crossed_y[...] = total.astype(BF16)
        for d in (2, 1, 3):
            yc_copy(d).start()

    def stage_crossed_y():
        for d in range(1, 4):
            yc_copy(d).wait_recv()
        total = crossed_y[y].astype(F32)
        for d in range(3):
            total += crossed_mine[d].astype(F32)
        share(CROSSED, total)

    def share(c, total):
        own = total.astype(BF16)
        own_rows[c] = own

        @pl.when(own_m)
        def _():
            mbuf[c, cc, x] = own

        @pl.when(own_n)
        def _():
            n_low[c, x, y_lo, cc] = own[:HALF]

        over_x[c, x] = own[HALF:]
        for d in (2, 1, 3):
            n_copy(c, d).start()
            xf_copy(c, d).start()

        @pl.when(jnp.logical_not(own_n))
        def _():
            n_copy(c, 0).start()

        for d in (2, 1, 3):
            m_copy(c, d).start()

        @pl.when(jnp.logical_not(own_m))
        def _():
            m_copy(c, 0).start()

    def each_foreign(body):
        for j in range(2):
            for pc in range(2):
                mine = jnp.logical_and(own_n, jnp.logical_and(y_lo == j, cc == pc))

                @pl.when(jnp.logical_not(mine))
                def _():
                    body(j, pc)

    def stage_relay(c):
        each_foreign(lambda j, pc: n_arrival(c, j, pc).wait_recv())
        for d in (2, 1, 3):
            nx_copy(c, d).start()
        for d in range(1, 4):
            xf_copy(c, d).wait_recv()
        for d in (2, 1, 3):
            xn_copy(c, d).start()

        @pl.when(own_n)
        def _():
            n_high[c, y_lo, cc] = over_x[c]

        @pl.when(jnp.logical_not(own_n))
        def _():
            xn_copy(c, 0).start()

    def stage_m(c):
        @pl.when(jnp.logical_not(own_m))
        def _():
            m_arrival(c, 0).wait_recv()

        for e in range(1, 4):
            m_arrival(c, e).wait_recv()
        relay(c).start()

    def stage_response(c):
        if c == 0:
            for d in range(1, 4):
                wx_copy(d).wait_recv()
        relay(c).wait_recv()
        groups = [(xs, pc) for xs in range(4) for pc in range(2)]
        left = jnp.concatenate(
            [
                (wbuf[xs, pc, c][:, None, :] * mbuf[c, pc, xs].astype(F32)[None])
                .astype(BF16)
                .reshape(512, 128)
                for xs, pc in groups
            ],
            axis=1,
        )
        for d in range(1, 4):
            nx_copy(c, d).wait_recv()
        each_foreign(lambda j, pc: xn_arrival(c, j, pc).wait_recv())
        right = jnp.concatenate(
            [
                jnp.concatenate(
                    [
                        part
                        for j in range(2)
                        for part in (n_low[c, xs, j, pc], n_high[c, j, pc, xs])
                    ],
                    axis=0,
                )
                for xs, pc in groups
            ],
            axis=1,
        )
        part = lax.dot_general(left, right, (((1,), (1,)), ((), ())), preferred_element_type=F32)
        if c == 0:
            acc[...] = part
        else:
            acc[...] += part

    def send_tile(j):
        rows = acc[...].reshape(8, 64, 128)[:, :, j * 64 : (j + 1) * 64]
        tile = jnp.concatenate([rows[:, :32], rows[:, 32:]], axis=2).astype(BF16)
        fsend[j] = tile
        mine = jnp.logical_and(own_c, y_lo == j)

        @pl.when(mine)
        def _():
            frecv[0] = tile

        @pl.when(jnp.logical_not(mine))
        def _():
            f_copy(j).start()

    pp_load(0).wait()
    for i, d in enumerate(row_order):
        zb = (zh + d) % 4
        basis_load(zb).wait()
        project_rows(0, zb)
        if i == 0:
            pl.semaphore_wait(barrier, expected)
        if d:
            zc_copy(d).start()
        send_y_part(0, zb)
    pp_load(1).wait()

    def second_rows(zb, carry):
        project_rows(1, zb)
        return carry

    lax.fori_loop(0, 4, second_rows, 0)
    send_y(2)
    send_y(3)
    make_weights()
    w_copy.start()
    stage_y(0)
    w_copy.wait_recv()
    for d in range(1, 4):
        wx_copy(d).start()
    stage_crossed_z()
    stage_y(2)
    stage_z(0)
    stage_y(3)
    stage_crossed_y()
    stage_z(2)
    stage_relay(0)
    stage_relay(1)
    stage_m(0)
    stage_z(3)
    stage_relay(2)
    stage_response(0)
    stage_m(1)
    stage_relay(3)
    stage_response(1)
    stage_m(2)
    stage_response(2)
    stage_m(3)
    stage_response(3)
    for j in range(2):
        send_tile(j)

    for c in range(CHUNKS):
        for d in range(1, 4):
            if c == CROSSED:
                zc_copy(d).wait_send()
                yc_copy(d).wait_send()
            else:
                y_copy(c, d).wait_send()
                z_copy(c, d).wait_send()
            m_copy(c, d).wait_send()
            n_copy(c, d).wait_send()
            nx_copy(c, d).wait_send()
            xf_copy(c, d).wait_send()
            xn_copy(c, d).wait_send()

        @pl.when(jnp.logical_not(own_n))
        def _():
            n_copy(c, 0).wait_send()
            xn_copy(c, 0).wait_send()

        @pl.when(jnp.logical_not(own_m))
        def _():
            m_copy(c, 0).wait_send()

        relay(c).wait_send()
    w_copy.wait_send()
    for d in range(1, 4):
        wx_copy(d).wait_send()

    @pl.when(jnp.logical_not(own_c))
    def _():
        f_arrival(0).wait_recv()

    f_arrival(1).wait_recv()
    total = frecv[0].astype(F32) + frecv[1].astype(F32)
    rows = jnp.concatenate([total[:, :, :64], total[:, :, 64:]], axis=1)
    out_ref[...] = jnp.swapaxes(rows, 1, 2)
    for j in range(2):
        mine = jnp.logical_and(own_c, y_lo == j)

        @pl.when(jnp.logical_not(mine))
        def _():
            f_copy(j).wait_send()


def per_device(
    pair_products, basis, val_energy, cond_energy, frequencies, valence_index, conduction_index
):
    pairs_total = pair_products.shape[1] * lax.axis_size("pair")
    vmem = pl.BlockSpec(memory_space=pltpu.VMEM)
    hbm = pl.BlockSpec(memory_space=pl.ANY)
    dma = pltpu.SemaphoreType.DMA
    return pl.pallas_call(
        functools.partial(kernel, pairs_total),
        out_shape=jax.ShapeDtypeStruct((8, 64, 64), F32),
        in_specs=[hbm] * 7,
        out_specs=vmem,
        scratch_shapes=[
            pltpu.VMEM((1, 128), F32),
            pltpu.VMEM((1, 128), F32),
            pltpu.SMEM((8,), F32),
            pltpu.VMEM((1, 512), jnp.int32),
            pltpu.VMEM((1, 512), jnp.int32),
            dma((5,)),
            pltpu.VMEM((4, 2048, 256), BF16),
            pltpu.VMEM((HALVES, 2048, 256), BF16),
            pltpu.VMEM((CHUNKS, 4, 4, 64, 128), BF16),
            pltpu.VMEM((CHUNKS, 3, 4, 64, 128), BF16),
            pltpu.VMEM((CHUNKS, 4, 64, 128), BF16),
            pltpu.VMEM((CHUNKS, 3, 64, 128), BF16),
            pltpu.VMEM((3, 4, 64, 128), BF16),
            pltpu.VMEM((4, 64, 128), BF16),
            pltpu.VMEM((3, 64, 128), BF16),
            pltpu.VMEM((CHUNKS, 64, 128), BF16),
            pltpu.VMEM((CHUNKS, 2, 4, 64, 128), BF16),
            pltpu.VMEM((CHUNKS, 4, 2, 2, HALF, 128), BF16),
            pltpu.VMEM((CHUNKS, 2, 2, 4, HALF, 128), BF16),
            pltpu.VMEM((CHUNKS, 4, HALF, 128), BF16),
            pltpu.VMEM((4, 2, CHUNKS, 8, 128), F32),
            pltpu.VMEM((512, 128), F32),
            pltpu.VMEM((2, 8, 32, 128), BF16),
            pltpu.VMEM((2, 8, 32, 128), BF16),
            dma((4,)),
            dma((HALVES,)),
            dma((CHUNKS, 3)),
            dma((CHUNKS, 3)),
            dma((CHUNKS, 3)),
            dma((CHUNKS, 3)),
            dma((CHUNKS, 4)),
            dma((CHUNKS, 4)),
            dma((CHUNKS, 4)),
            dma((CHUNKS, 4)),
            dma((CHUNKS, 3)),
            dma((CHUNKS, 3)),
            dma((CHUNKS, 3)),
            dma((CHUNKS, 3)),
            dma((CHUNKS, 4)),
            dma((CHUNKS, 4)),
            dma((CHUNKS,)),
            dma((CHUNKS,)),
            dma(()),
            dma(()),
            dma((3,)),
            dma((3,)),
            dma((2,)),
            dma((2,)),
        ],
        compiler_params=pltpu.CompilerParams(
            collective_id=0, has_side_effects=True, vmem_limit_bytes=56 * 2**20
        ),
    )(
        pair_products,
        basis,
        val_energy.reshape(1, -1),
        cond_energy.reshape(1, -1),
        frequencies,
        valence_index.reshape(1, -1),
        conduction_index.reshape(1, -1),
    )


def solution(mesh):
    placed = (P("pw", "pair"), P("pw", None), P(), P(), P(), P("pair"), P("pair"))
    return jax.shard_map(
        per_device, mesh=mesh, in_specs=placed, out_specs=P(None, "pw", "pair"), check_vma=False
    )
```

```python
import functools

import jax
import jax.numpy as jnp
from jax import lax
from jax.experimental import pallas as pl
from jax.experimental.pallas import tpu as pltpu
from jax.sharding import PartitionSpec as P

F32 = jnp.float32
BF16 = jnp.bfloat16
MESH = pl.DeviceIdType.MESH
CHUNKS = 4
CROSSED = 1
HALF = 32
HALVES = 2


def kernel(
    pairs_total,
    pp_hbm,
    basis_hbm,
    val_hbm,
    cond_hbm,
    freq_hbm,
    vidx_hbm,
    cidx_hbm,
    out_ref,
    val_ref,
    cond_ref,
    freq_ref,
    vidx_ref,
    cidx_ref,
    small_sem,
    ready_sem,
    basis_v,
    pp_v,
    psend,
    yrecv,
    zsend,
    zrecv,
    crossed_z,
    crossed_y,
    crossed_mine,
    own_rows,
    mbuf,
    n_low,
    n_high,
    over_x,
    wbuf,
    acc,
    fsend,
    frecv,
    basis_sem,
    pp_sem,
    y_ss,
    y_rs,
    z_ss,
    z_rs,
    m_ss,
    m_rs,
    n_ss,
    n_rs,
    nx_ss,
    nx_rs,
    xf_ss,
    xf_rs,
    xn_ss,
    xn_rs,
    r_ss,
    r_rs,
    w_ss,
    w_rs,
    wx_ss,
    wx_rs,
    f_ss,
    f_rs,
):
    pair, pw = lax.axis_index("pair"), lax.axis_index("pw")
    x, zl, cc = pair // 4, (pair // 2) % 2, pair % 2
    zh, y = pw // 4, pw % 4
    y_hi, y_lo = y // 2, y % 2

    def dev(x=x, zl=zl, cc=cc, zh=zh, y=y):
        return {"pair": x * 4 + zl * 2 + cc, "pw": zh * 4 + y}

    def basis_load(zb):
        return pltpu.make_async_copy(
            basis_hbm.at[:, pl.ds(pl.multiple_of(zb * 256, 256), 256)],
            basis_v.at[zb],
            basis_sem.at[zb],
        )

    def pp_load(h):
        return pltpu.make_async_copy(
            pp_hbm.at[:, pl.ds(h * 256, 256)], pp_v.at[h], pp_sem.at[h]
        )

    pp_load(0).start()
    row_order = (2, 1, 3, 0)
    for d in row_order:
        basis_load((zh + d) % 4).start()
    pp_load(1).start()
    small_loads = [
        pltpu.make_async_copy(source, target, small_sem.at[i])
        for i, (source, target) in enumerate(
            [
                (val_hbm, val_ref),
                (cond_hbm, cond_ref),
                (freq_hbm, freq_ref),
                (vidx_hbm, vidx_ref),
                (cidx_hbm, cidx_ref),
            ]
        )
    ]
    for load in small_loads:
        load.start()

    own_n = y_hi == cc
    own_m = x == zh
    own_c = jnp.logical_and(y == 2 * zl + cc, y_hi == cc)
    barrier = pltpu.get_barrier_semaphore()

    def greet(device):
        pl.semaphore_signal(barrier, inc=1, device_id=device, device_id_type=MESH)

    for d in range(1, 4):
        greet(dev(y=(y + 4 - d) % 4))
        greet(dev(zh=(zh + 4 - d) % 4))
        greet(dev(x=(x + 4 - d) % 4))
    greet(dev(cc=1 - cc))
    greet(dev(zl=1 - zl))
    expected = 11

    def y_copy(c, d):
        return pltpu.make_async_remote_copy(
            src_ref=psend.at[c, (y + d) % 4],
            dst_ref=yrecv.at[c, d - 1],
            send_sem=y_ss.at[c, d - 1],
            recv_sem=y_rs.at[c, d - 1],
            device_id=dev(y=(y + d) % 4),
            device_id_type=MESH,
        )

    def y_part(c, d, zb):
        return pltpu.make_async_remote_copy(
            src_ref=psend.at[c, (y + d) % 4, zb],
            dst_ref=yrecv.at[c, d - 1, zb],
            send_sem=y_ss.at[c, d - 1],
            recv_sem=y_rs.at[c, d - 1],
            device_id=dev(y=(y + d) % 4),
            device_id_type=MESH,
        )

    def z_copy(c, d):
        return pltpu.make_async_remote_copy(
            src_ref=zsend.at[c, (zh + d) % 4],
            dst_ref=zrecv.at[c, d - 1],
            send_sem=z_ss.at[c, d - 1],
            recv_sem=z_rs.at[c, d - 1],
            device_id=dev(zh=(zh + d) % 4),
            device_id_type=MESH,
        )

    def zc_copy(d):
        return pltpu.make_async_remote_copy(
            src_ref=psend.at[CROSSED, :, (zh + d) % 4],
            dst_ref=crossed_z.at[d - 1],
            send_sem=z_ss.at[CROSSED, d - 1],
            recv_sem=z_rs.at[CROSSED, d - 1],
            device_id=dev(zh=(zh + d) % 4),
            device_id_type=MESH,
        )

    def yc_copy(d):
        return pltpu.make_async_remote_copy(
            src_ref=crossed_y.at[(y + d) % 4],
            dst_ref=crossed_mine.at[d - 1],
            send_sem=y_ss.at[CROSSED, d - 1],
            recv_sem=y_rs.at[CROSSED, d - 1],
            device_id=dev(y=(y + d) % 4),
            device_id_type=MESH,
        )

    def m_copy(c, d):
        return pltpu.make_async_remote_copy(
            src_ref=own_rows.at[c],
            dst_ref=mbuf.at[c, cc, x],
            send_sem=m_ss.at[c, d],
            recv_sem=m_rs.at[c, x],
            device_id=dev(x=zh, zh=(zh + d) % 4),
            device_id_type=MESH,
        )

    def m_arrival(c, e):
        return pltpu.make_async_remote_copy(
            src_ref=own_rows.at[c],
            dst_ref=mbuf.at[c, cc, (x + e) % 4],
            send_sem=m_ss.at[c, 0],
            recv_sem=m_rs.at[c, (x + e) % 4],
            device_id=dev(cc=1 - cc),
            device_id_type=MESH,
        )

    low, high = pl.ds(0, HALF), pl.ds(HALF, HALF)

    def remote(source, target, send_sem, recv_sem, device):
        return pltpu.make_async_remote_copy(
            src_ref=source,
            dst_ref=target,
            send_sem=send_sem,
            recv_sem=recv_sem,
            device_id=device,
            device_id_type=MESH,
        )

    sibling = dev(cc=1 - cc)

    def n_copy(c, d):
        return remote(
            own_rows.at[c, low],
            n_low.at[c, x, y_lo, cc],
            n_ss.at[c, d],
            n_rs.at[c, y_lo * 2 + cc],
            dev(y=(y + d) % 4, cc=y_hi),
        )

    def n_arrival(c, j, pc):
        return remote(
            own_rows.at[c, low],
            n_low.at[c, x, j, pc],
            n_ss.at[c, 0],
            n_rs.at[c, j * 2 + pc],
            sibling,
        )

    def nx_copy(c, d):
        return remote(
            n_low.at[c, x],
            n_low.at[c, x],
            nx_ss.at[c, d - 1],
            nx_rs.at[c, d - 1],
            dev(x=(x + d) % 4),
        )

    def xf_copy(c, d):
        return remote(
            own_rows.at[c, high],
            over_x.at[c, x],
            xf_ss.at[c, d - 1],
            xf_rs.at[c, d - 1],
            dev(x=(x + d) % 4),
        )

    def xn_copy(c, d):
        return remote(
            over_x.at[c],
            n_high.at[c, y_lo, cc],
            xn_ss.at[c, d],
            xn_rs.at[c, y_lo * 2 + cc],
            dev(y=(y + d) % 4, cc=y_hi),
        )

    def xn_arrival(c, j, pc):
        return remote(
            over_x.at[c],
            n_high.at[c, j, pc],
            xn_ss.at[c, 0],
            xn_rs.at[c, j * 2 + pc],
            sibling,
        )

    def relay(c):
        return pltpu.make_async_remote_copy(
            src_ref=mbuf.at[c, cc],
            dst_ref=mbuf.at[c, cc],
            send_sem=r_ss.at[c],
            recv_sem=r_rs.at[c],
            device_id=dev(cc=1 - cc),
            device_id_type=MESH,
        )

    def wx_copy(d):
        return pltpu.make_async_remote_copy(
            src_ref=wbuf.at[x],
            dst_ref=wbuf.at[x],
            send_sem=wx_ss.at[d - 1],
            recv_sem=wx_rs.at[d - 1],
            device_id=dev(x=(x + d) % 4),
            device_id_type=MESH,
        )

    w_copy = pltpu.make_async_remote_copy(
        src_ref=wbuf.at[x, cc],
        dst_ref=wbuf.at[x, cc],
        send_sem=w_ss,
        recv_sem=w_rs,
        device_id=dev(cc=1 - cc),
        device_id_type=MESH,
    )

    def f_copy(j, q):
        slot = (y_hi + zl) % 2
        ks = pl.ds(q * 4, 4)
        return remote(
            fsend.at[j, ks],
            frecv.at[slot, ks],
            f_ss.at[j, q],
            f_rs.at[slot, q],
            dev(y=2 * cc + j, zl=y_hi, cc=y_lo),
        )

    def f_arrival(slot, q):
        ks = pl.ds(q * 4, 4)
        return remote(
            fsend.at[0, ks], frecv.at[slot, ks], f_ss.at[0, q], f_rs.at[slot, q], sibling
        )

    def project_rows(h, zb):
        block = lax.dot_general(
            basis_v[zb], pp_v[h], (((0,), (0,)), ((), ())), preferred_element_type=F32
        )
        block = block.astype(BF16).reshape(4, 64, 256)
        psend[2 * h, :, zb] = block[:, :, :128]
        psend[2 * h + 1, :, zb] = block[:, :, 128:]

    def send_y(c):
        for d in (2, 1, 3):
            y_copy(c, d).start()

    def send_y_part(c, zb):
        for d in (2, 1, 3):
            y_part(c, d, zb).start()

    def make_weights():
        for load in small_loads:
            load.wait()
        levels = lax.broadcasted_iota(jnp.int32, (128, 512), 0)

        def lookup(index, table):
            column = jnp.transpose(jnp.broadcast_to(table, (128, 128)))[:, :1]
            return jnp.sum(jnp.where(levels == index, column, 0.0), axis=0, keepdims=True)

        gap = lookup(cidx_ref[...], cond_ref[...]) - lookup(vidx_ref[...], val_ref[...])
        for k in range(8):
            freq = freq_ref[k]
            weight = -4.0 * gap / (gap * gap + freq * freq) / pairs_total
            for c in range(CHUNKS):
                wbuf[x, cc, c, k : k + 1, :] = weight[:, c * 128 : (c + 1) * 128]

    def stage_y(c):
        for d in range(1, 4):
            y_copy(c, d).wait_recv()
        total = psend[c, y].astype(F32)
        for d in range(3):
            total += yrecv[c, d].astype(F32)
        zsend[c] = total.astype(BF16)
        for d in (2, 1, 3):
            z_copy(c, d).start()

    def stage_z(c):
        for d in range(1, 4):
            z_copy(c, d).wait_recv()
        total = zsend[c, zh].astype(F32)
        for d in range(3):
            total += zrecv[c, d].astype(F32)
        share(c, total)

    def stage_crossed_z():
        for d in range(1, 4):
            zc_copy(d).wait_recv()
        total = psend[CROSSED, :, zh].astype(F32)
        for d in range(3):
            total += crossed_z[d].astype(F32)
        crossed_y[...] = total.astype(BF16)
        for d in (2, 1, 3):
            yc_copy(d).start()

    def stage_crossed_y():
        for d in range(1, 4):
            yc_copy(d).wait_recv()
        total = crossed_y[y].astype(F32)
        for d in range(3):
            total += crossed_mine[d].astype(F32)
        share(CROSSED, total)

    def share(c, total):
        if c == 0:
            pl.semaphore_wait(ready_sem, 6)
        own = total.astype(BF16)
        own_rows[c] = own

        @pl.when(own_m)
        def _():
            mbuf[c, cc, x] = own

        @pl.when(own_n)
        def _():
            n_low[c, x, y_lo, cc] = own[:HALF]

        over_x[c, x] = own[HALF:]
        for d in (2, 1, 3):
            n_copy(c, d).start()
            xf_copy(c, d).start()

        @pl.when(jnp.logical_not(own_n))
        def _():
            n_copy(c, 0).start()

        for d in (2, 1, 3):
            m_copy(c, d).start()

        @pl.when(jnp.logical_not(own_m))
        def _():
            m_copy(c, 0).start()

    def each_foreign(body):
        for j in range(2):
            for pc in range(2):
                mine = jnp.logical_and(own_n, jnp.logical_and(y_lo == j, cc == pc))

                @pl.when(jnp.logical_not(mine))
                def _():
                    body(j, pc)

    def stage_relay(c):
        each_foreign(lambda j, pc: n_arrival(c, j, pc).wait_recv())
        for d in (2, 1, 3):
            nx_copy(c, d).start()
        for d in range(1, 4):
            xf_copy(c, d).wait_recv()
        for d in (2, 1, 3):
            xn_copy(c, d).start()

        @pl.when(own_n)
        def _():
            n_high[c, y_lo, cc] = over_x[c]

        @pl.when(jnp.logical_not(own_n))
        def _():
            xn_copy(c, 0).start()

    def stage_m(c):
        @pl.when(jnp.logical_not(own_m))
        def _():
            m_arrival(c, 0).wait_recv()

        for e in range(1, 4):
            m_arrival(c, e).wait_recv()
        relay(c).start()

    def stage_response(c):
        if c == 0:
            for d in range(1, 4):
                wx_copy(d).wait_recv()
        relay(c).wait_recv()
        groups = [(xs, pc) for xs in range(4) for pc in range(2)]
        left = jnp.concatenate(
            [
                (wbuf[xs, pc, c][:, None, :] * mbuf[c, pc, xs].astype(F32)[None])
                .astype(BF16)
                .reshape(512, 128)
                for xs, pc in groups
            ],
            axis=1,
        )
        for d in range(1, 4):
            nx_copy(c, d).wait_recv()
        each_foreign(lambda j, pc: xn_arrival(c, j, pc).wait_recv())
        right = jnp.concatenate(
            [
                jnp.concatenate(
                    [
                        part
                        for j in range(2)
                        for part in (n_low[c, xs, j, pc], n_high[c, j, pc, xs])
                    ],
                    axis=0,
                )
                for xs, pc in groups
            ],
            axis=1,
        )
        if c < CHUNKS - 1:
            part = lax.dot_general(
                left, right, (((1,), (1,)), ((), ())), preferred_element_type=F32
            )
            if c == 0:
                acc[...] = part
            else:
                acc[...] += part
        else:
            for q in range(2):
                part = lax.dot_general(
                    left[q * 256 : (q + 1) * 256],
                    right,
                    (((1,), (1,)), ((), ())),
                    preferred_element_type=F32,
                )
                send_tiles(q, acc[q * 256 : (q + 1) * 256] + part)

    def send_tiles(q, total):
        ks = pl.ds(q * 4, 4)
        for j in range(2):
            rows = total.reshape(4, 64, 128)[:, :, j * 64 : (j + 1) * 64]
            tile = jnp.concatenate([rows[:, :32], rows[:, 32:]], axis=2).astype(BF16)
            fsend[j, ks] = tile
            mine = jnp.logical_and(own_c, y_lo == j)

            @pl.when(mine)
            def _():
                frecv[0, ks] = tile

            @pl.when(jnp.logical_not(mine))
            def _():
                f_copy(j, q).start()

    pp_load(0).wait()
    for i, d in enumerate(row_order):
        zb = (zh + d) % 4
        basis_load(zb).wait()
        project_rows(0, zb)
        if i == 0:
            pl.semaphore_wait(barrier, expected)
            for step in range(1, 4):
                for peer in (dev(y=(y + step) % 4), dev(zh=(zh + step) % 4)):
                    pl.semaphore_signal(
                        ready_sem, inc=1, device_id=peer, device_id_type=MESH
                    )
        if d:
            zc_copy(d).start()
        send_y_part(0, zb)
    pp_load(1).wait()

    def second_rows(zb, carry):
        project_rows(1, zb)
        return carry

    lax.fori_loop(0, 4, second_rows, 0, unroll=True)
    send_y(2)
    send_y(3)
    make_weights()
    w_copy.start()
    stage_y(0)
    w_copy.wait_recv()
    for d in range(1, 4):
        wx_copy(d).start()
    stage_crossed_z()
    stage_y(2)
    stage_z(0)
    stage_y(3)
    stage_crossed_y()
    stage_z(2)
    stage_relay(0)
    stage_relay(1)
    stage_m(0)
    stage_z(3)
    stage_relay(2)
    stage_response(0)
    stage_m(1)
    stage_relay(3)
    stage_response(1)
    stage_m(2)
    stage_response(2)
    stage_m(3)
    stage_response(3)
    for c in range(CHUNKS):
        for d in range(1, 4):
            if c == CROSSED:
                zc_copy(d).wait_send()
                yc_copy(d).wait_send()
            else:
                y_copy(c, d).wait_send()
                z_copy(c, d).wait_send()
            m_copy(c, d).wait_send()
            n_copy(c, d).wait_send()
            nx_copy(c, d).wait_send()
            xf_copy(c, d).wait_send()
            xn_copy(c, d).wait_send()

        @pl.when(jnp.logical_not(own_n))
        def _():
            n_copy(c, 0).wait_send()
            xn_copy(c, 0).wait_send()

        @pl.when(jnp.logical_not(own_m))
        def _():
            m_copy(c, 0).wait_send()

        relay(c).wait_send()
    w_copy.wait_send()
    for d in range(1, 4):
        wx_copy(d).wait_send()

    for q in range(2):
        ks = pl.ds(q * 4, 4)

        @pl.when(jnp.logical_not(own_c))
        def _():
            f_arrival(0, q).wait_recv()

        f_arrival(1, q).wait_recv()
        total = frecv[0, ks].astype(F32) + frecv[1, ks].astype(F32)
        rows = jnp.concatenate([total[:, :, :64], total[:, :, 64:]], axis=1)
        out_ref[ks] = jnp.swapaxes(rows, 1, 2)
    for j in range(2):
        mine = jnp.logical_and(own_c, y_lo == j)

        @pl.when(jnp.logical_not(mine))
        def _():
            for q in range(2):
                f_copy(j, q).wait_send()


def per_device(
    pair_products, basis, val_energy, cond_energy, frequencies, valence_index, conduction_index
):
    pairs_total = pair_products.shape[1] * lax.axis_size("pair")
    vmem = pl.BlockSpec(memory_space=pltpu.VMEM)
    hbm = pl.BlockSpec(memory_space=pl.ANY)
    dma = pltpu.SemaphoreType.DMA
    return pl.pallas_call(
        functools.partial(kernel, pairs_total),
        out_shape=jax.ShapeDtypeStruct((8, 64, 64), F32),
        in_specs=[hbm] * 7,
        out_specs=vmem,
        scratch_shapes=[
            pltpu.VMEM((1, 128), F32),
            pltpu.VMEM((1, 128), F32),
            pltpu.SMEM((8,), F32),
            pltpu.VMEM((1, 512), jnp.int32),
            pltpu.VMEM((1, 512), jnp.int32),
            dma((5,)),
            pltpu.SemaphoreType.REGULAR,
            pltpu.VMEM((4, 2048, 256), BF16),
            pltpu.VMEM((HALVES, 2048, 256), BF16),
            pltpu.VMEM((CHUNKS, 4, 4, 64, 128), BF16),
            pltpu.VMEM((CHUNKS, 3, 4, 64, 128), BF16),
            pltpu.VMEM((CHUNKS, 4, 64, 128), BF16),
            pltpu.VMEM((CHUNKS, 3, 64, 128), BF16),
            pltpu.VMEM((3, 4, 64, 128), BF16),
            pltpu.VMEM((4, 64, 128), BF16),
            pltpu.VMEM((3, 64, 128), BF16),
            pltpu.VMEM((CHUNKS, 64, 128), BF16),
            pltpu.VMEM((CHUNKS, 2, 4, 64, 128), BF16),
            pltpu.VMEM((CHUNKS, 4, 2, 2, HALF, 128), BF16),
            pltpu.VMEM((CHUNKS, 2, 2, 4, HALF, 128), BF16),
            pltpu.VMEM((CHUNKS, 4, HALF, 128), BF16),
            pltpu.VMEM((4, 2, CHUNKS, 8, 128), F32),
            pltpu.VMEM((512, 128), F32),
            pltpu.VMEM((2, 8, 32, 128), BF16),
            pltpu.VMEM((2, 8, 32, 128), BF16),
            dma((4,)),
            dma((HALVES,)),
            dma((CHUNKS, 3)),
            dma((CHUNKS, 3)),
            dma((CHUNKS, 3)),
            dma((CHUNKS, 3)),
            dma((CHUNKS, 4)),
            dma((CHUNKS, 4)),
            dma((CHUNKS, 4)),
            dma((CHUNKS, 4)),
            dma((CHUNKS, 3)),
            dma((CHUNKS, 3)),
            dma((CHUNKS, 3)),
            dma((CHUNKS, 3)),
            dma((CHUNKS, 4)),
            dma((CHUNKS, 4)),
            dma((CHUNKS,)),
            dma((CHUNKS,)),
            dma(()),
            dma(()),
            dma((3,)),
            dma((3,)),
            dma((2, 2)),
            dma((2, 2)),
        ],
        compiler_params=pltpu.CompilerParams(
            collective_id=0, has_side_effects=True, vmem_limit_bytes=56 * 2**20
        ),
    )(
        pair_products,
        basis,
        val_energy.reshape(1, -1),
        cond_energy.reshape(1, -1),
        frequencies,
        valence_index.reshape(1, -1),
        conduction_index.reshape(1, -1),
    )


def solution(mesh):
    placed = (P("pw", "pair"), P("pw", None), P(), P(), P(), P("pair"), P("pair"))
    return jax.shard_map(
        per_device, mesh=mesh, in_specs=placed, out_specs=P(None, "pw", "pair"), check_vma=False
    )
```

```python
import functools

import jax
import jax.numpy as jnp
from jax import lax
from jax.experimental import pallas as pl
from jax.experimental.pallas import tpu as pltpu
from jax.sharding import PartitionSpec as P

F32 = jnp.float32
BF16 = jnp.bfloat16
MESH = pl.DeviceIdType.MESH
CHUNKS = 4
CROSSED = 1
HALF = 32
HALVES = 2


def kernel(
    pairs_total,
    pp_hbm,
    basis_hbm,
    val_hbm,
    cond_hbm,
    freq_hbm,
    vidx_hbm,
    cidx_hbm,
    out_ref,
    val_ref,
    cond_ref,
    freq_ref,
    vidx_ref,
    cidx_ref,
    small_sem,
    ready_sem,
    basis_v,
    pp_v,
    psend,
    yrecv,
    zsend,
    zrecv,
    crossed_z,
    crossed_y,
    crossed_mine,
    own_rows,
    mbuf,
    n_low,
    n_high,
    over_x,
    wbuf,
    acc,
    fsend,
    frecv,
    basis_sem,
    pp_sem,
    y_ss,
    y_rs,
    z_ss,
    z_rs,
    m_ss,
    m_rs,
    n_ss,
    n_rs,
    nx_ss,
    nx_rs,
    xf_ss,
    xf_rs,
    xn_ss,
    xn_rs,
    r_ss,
    r_rs,
    w_ss,
    w_rs,
    wx_ss,
    wx_rs,
    f_ss,
    f_rs,
):
    pair, pw = lax.axis_index("pair"), lax.axis_index("pw")
    x, zl, cc = pair // 4, (pair // 2) % 2, pair % 2
    zh, y = pw // 4, pw % 4
    y_hi, y_lo = y // 2, y % 2

    def dev(x=x, zl=zl, cc=cc, zh=zh, y=y):
        return {"pair": x * 4 + zl * 2 + cc, "pw": zh * 4 + y}

    def basis_load(zb):
        return pltpu.make_async_copy(
            basis_hbm.at[:, pl.ds(pl.multiple_of(zb * 256, 256), 256)],
            basis_v.at[zb],
            basis_sem.at[zb],
        )

    def pp_load(h):
        return pltpu.make_async_copy(
            pp_hbm.at[:, pl.ds(h * 256, 256)], pp_v.at[h], pp_sem.at[h]
        )

    pp_load(0).start()
    row_order = (2, 1, 3, 0)
    for d in row_order:
        basis_load((zh + d) % 4).start()
    pp_load(1).start()
    small_loads = [
        pltpu.make_async_copy(source, target, small_sem.at[i])
        for i, (source, target) in enumerate(
            [
                (val_hbm, val_ref),
                (cond_hbm, cond_ref),
                (freq_hbm, freq_ref),
                (vidx_hbm, vidx_ref),
                (cidx_hbm, cidx_ref),
            ]
        )
    ]
    for load in small_loads:
        load.start()

    own_n = y_hi == cc
    own_m = x == zh
    own_c = jnp.logical_and(y == 2 * zl + cc, y_hi == cc)
    barrier = pltpu.get_barrier_semaphore()

    def greet(device):
        pl.semaphore_signal(barrier, inc=1, device_id=device, device_id_type=MESH)

    for d in range(1, 4):
        greet(dev(y=(y + 4 - d) % 4))
        greet(dev(zh=(zh + 4 - d) % 4))
        greet(dev(x=(x + 4 - d) % 4))
    greet(dev(cc=1 - cc))
    greet(dev(zl=1 - zl))
    expected = 11

    def y_copy(c, d):
        return pltpu.make_async_remote_copy(
            src_ref=psend.at[c, (y + d) % 4],
            dst_ref=yrecv.at[c, d - 1],
            send_sem=y_ss.at[c, d - 1],
            recv_sem=y_rs.at[c, d - 1],
            device_id=dev(y=(y + d) % 4),
            device_id_type=MESH,
        )

    def y_part(c, d, zb):
        return pltpu.make_async_remote_copy(
            src_ref=psend.at[c, (y + d) % 4, zb],
            dst_ref=yrecv.at[c, d - 1, zb],
            send_sem=y_ss.at[c, d - 1],
            recv_sem=y_rs.at[c, d - 1],
            device_id=dev(y=(y + d) % 4),
            device_id_type=MESH,
        )

    def z_copy(c, d):
        return pltpu.make_async_remote_copy(
            src_ref=zsend.at[c, (zh + d) % 4],
            dst_ref=zrecv.at[c, d - 1],
            send_sem=z_ss.at[c, d - 1],
            recv_sem=z_rs.at[c, d - 1],
            device_id=dev(zh=(zh + d) % 4),
            device_id_type=MESH,
        )

    def zc_copy(d):
        return pltpu.make_async_remote_copy(
            src_ref=psend.at[CROSSED, :, (zh + d) % 4],
            dst_ref=crossed_z.at[d - 1],
            send_sem=z_ss.at[CROSSED, d - 1],
            recv_sem=z_rs.at[CROSSED, d - 1],
            device_id=dev(zh=(zh + d) % 4),
            device_id_type=MESH,
        )

    def yc_copy(d):
        return pltpu.make_async_remote_copy(
            src_ref=crossed_y.at[(y + d) % 4],
            dst_ref=crossed_mine.at[d - 1],
            send_sem=y_ss.at[CROSSED, d - 1],
            recv_sem=y_rs.at[CROSSED, d - 1],
            device_id=dev(y=(y + d) % 4),
            device_id_type=MESH,
        )

    def m_copy(c, d):
        return pltpu.make_async_remote_copy(
            src_ref=own_rows.at[c],
            dst_ref=mbuf.at[c, cc, x],
            send_sem=m_ss.at[c, d],
            recv_sem=m_rs.at[c, x],
            device_id=dev(x=zh, zh=(zh + d) % 4),
            device_id_type=MESH,
        )

    def m_arrival(c, e):
        return pltpu.make_async_remote_copy(
            src_ref=own_rows.at[c],
            dst_ref=mbuf.at[c, cc, (x + e) % 4],
            send_sem=m_ss.at[c, 0],
            recv_sem=m_rs.at[c, (x + e) % 4],
            device_id=dev(cc=1 - cc),
            device_id_type=MESH,
        )

    low, high = pl.ds(0, HALF), pl.ds(HALF, HALF)

    def remote(source, target, send_sem, recv_sem, device):
        return pltpu.make_async_remote_copy(
            src_ref=source,
            dst_ref=target,
            send_sem=send_sem,
            recv_sem=recv_sem,
            device_id=device,
            device_id_type=MESH,
        )

    sibling = dev(cc=1 - cc)

    def n_copy(c, d):
        return remote(
            own_rows.at[c, low],
            n_low.at[c, x, y_lo, cc],
            n_ss.at[c, d],
            n_rs.at[c, y_lo * 2 + cc],
            dev(y=(y + d) % 4, cc=y_hi),
        )

    def n_arrival(c, j, pc):
        return remote(
            own_rows.at[c, low],
            n_low.at[c, x, j, pc],
            n_ss.at[c, 0],
            n_rs.at[c, j * 2 + pc],
            sibling,
        )

    def nx_copy(c, d):
        return remote(
            n_low.at[c, x],
            n_low.at[c, x],
            nx_ss.at[c, d - 1],
            nx_rs.at[c, d - 1],
            dev(x=(x + d) % 4),
        )

    def xf_copy(c, d):
        return remote(
            own_rows.at[c, high],
            over_x.at[c, x],
            xf_ss.at[c, d - 1],
            xf_rs.at[c, d - 1],
            dev(x=(x + d) % 4),
        )

    def xn_copy(c, d):
        return remote(
            over_x.at[c],
            n_high.at[c, y_lo, cc],
            xn_ss.at[c, d],
            xn_rs.at[c, y_lo * 2 + cc],
            dev(y=(y + d) % 4, cc=y_hi),
        )

    def xn_arrival(c, j, pc):
        return remote(
            over_x.at[c],
            n_high.at[c, j, pc],
            xn_ss.at[c, 0],
            xn_rs.at[c, j * 2 + pc],
            sibling,
        )

    def relay(c):
        return pltpu.make_async_remote_copy(
            src_ref=mbuf.at[c, cc],
            dst_ref=mbuf.at[c, cc],
            send_sem=r_ss.at[c],
            recv_sem=r_rs.at[c],
            device_id=dev(cc=1 - cc),
            device_id_type=MESH,
        )

    def wx_copy(d):
        return pltpu.make_async_remote_copy(
            src_ref=wbuf.at[x],
            dst_ref=wbuf.at[x],
            send_sem=wx_ss.at[d - 1],
            recv_sem=wx_rs.at[d - 1],
            device_id=dev(x=(x + d) % 4),
            device_id_type=MESH,
        )

    w_copy = pltpu.make_async_remote_copy(
        src_ref=wbuf.at[x, cc],
        dst_ref=wbuf.at[x, cc],
        send_sem=w_ss,
        recv_sem=w_rs,
        device_id=dev(cc=1 - cc),
        device_id_type=MESH,
    )

    def f_copy(j, q):
        slot = (y_hi + zl) % 2
        ks = pl.ds(q * 4, 4)
        return remote(
            fsend.at[j, ks],
            frecv.at[slot, ks],
            f_ss.at[j, q],
            f_rs.at[slot, q],
            dev(y=2 * cc + j, zl=y_hi, cc=y_lo),
        )

    def f_arrival(slot, q):
        ks = pl.ds(q * 4, 4)
        return remote(
            fsend.at[0, ks], frecv.at[slot, ks], f_ss.at[0, q], f_rs.at[slot, q], sibling
        )

    def project_rows(h, zb):
        block = lax.dot_general(
            basis_v[zb], pp_v[h], (((0,), (0,)), ((), ())), preferred_element_type=F32
        )
        block = block.astype(BF16).reshape(4, 64, 256)
        psend[2 * h, :, zb] = block[:, :, :128]
        psend[2 * h + 1, :, zb] = block[:, :, 128:]

    def send_y(c):
        for d in (2, 1, 3):
            y_copy(c, d).start()

    def send_y_part(c, zb):
        for d in (2, 1, 3):
            y_part(c, d, zb).start()

    def make_weights():
        for load in small_loads:
            load.wait()
        levels = lax.broadcasted_iota(jnp.int32, (128, 512), 0)

        def lookup(index, table):
            column = jnp.transpose(jnp.broadcast_to(table, (128, 128)))[:, :1]
            return jnp.sum(jnp.where(levels == index, column, 0.0), axis=0, keepdims=True)

        gap = lookup(cidx_ref[...], cond_ref[...]) - lookup(vidx_ref[...], val_ref[...])
        for k in range(8):
            freq = freq_ref[k]
            weight = -4.0 * gap / (gap * gap + freq * freq) / pairs_total
            for c in range(CHUNKS):
                wbuf[x, cc, c, k : k + 1, :] = weight[:, c * 128 : (c + 1) * 128]

    def stage_y(c):
        for d in range(1, 4):
            y_copy(c, d).wait_recv()
        total = psend[c, y].astype(F32)
        for d in range(3):
            total += yrecv[c, d].astype(F32)
        zsend[c] = total.astype(BF16)
        for d in (2, 1, 3):
            z_copy(c, d).start()

    def stage_z(c):
        for d in range(1, 4):
            z_copy(c, d).wait_recv()
        total = zsend[c, zh].astype(F32)
        for d in range(3):
            total += zrecv[c, d].astype(F32)
        share(c, total)

    def stage_crossed_z():
        for d in range(1, 4):
            zc_copy(d).wait_recv()
        total = psend[CROSSED, :, zh].astype(F32)
        for d in range(3):
            total += crossed_z[d].astype(F32)
        crossed_y[...] = total.astype(BF16)
        for d in (2, 1, 3):
            yc_copy(d).start()

    def stage_crossed_y():
        for d in range(1, 4):
            yc_copy(d).wait_recv()
        total = crossed_y[y].astype(F32)
        for d in range(3):
            total += crossed_mine[d].astype(F32)
        share(CROSSED, total)

    def share(c, total):
        if c == 0:
            pl.semaphore_wait(ready_sem, 6)
        own = total.astype(BF16)
        own_rows[c] = own

        @pl.when(own_m)
        def _():
            mbuf[c, cc, x] = own

        @pl.when(own_n)
        def _():
            n_low[c, x, y_lo, cc] = own[:HALF]

        over_x[c, x] = own[HALF:]
        for d in (2, 1, 3):
            n_copy(c, d).start()
            xf_copy(c, d).start()

        @pl.when(jnp.logical_not(own_n))
        def _():
            n_copy(c, 0).start()

        for d in (2, 1, 3):
            m_copy(c, d).start()

        @pl.when(jnp.logical_not(own_m))
        def _():
            m_copy(c, 0).start()

    def each_foreign(body):
        for j in range(2):
            for pc in range(2):
                mine = jnp.logical_and(own_n, jnp.logical_and(y_lo == j, cc == pc))

                @pl.when(jnp.logical_not(mine))
                def _():
                    body(j, pc)

    def stage_relay(c):
        each_foreign(lambda j, pc: n_arrival(c, j, pc).wait_recv())
        for d in (2, 1, 3):
            nx_copy(c, d).start()
        for d in range(1, 4):
            xf_copy(c, d).wait_recv()
        for d in (2, 1, 3):
            xn_copy(c, d).start()

        @pl.when(own_n)
        def _():
            n_high[c, y_lo, cc] = over_x[c]

        @pl.when(jnp.logical_not(own_n))
        def _():
            xn_copy(c, 0).start()

    def stage_m(c):
        @pl.when(jnp.logical_not(own_m))
        def _():
            m_arrival(c, 0).wait_recv()

        for e in range(1, 4):
            m_arrival(c, e).wait_recv()
        relay(c).start()

    def stage_response(c):
        if c == 0:
            for d in range(1, 4):
                wx_copy(d).wait_recv()
        relay(c).wait_recv()
        groups = [(xs, pc) for xs in range(4) for pc in range(2)]
        left = jnp.concatenate(
            [
                (wbuf[xs, pc, c][:, None, :] * mbuf[c, pc, xs].astype(F32)[None])
                .astype(BF16)
                .reshape(512, 128)
                for xs, pc in groups
            ],
            axis=1,
        )
        for d in range(1, 4):
            nx_copy(c, d).wait_recv()
        each_foreign(lambda j, pc: xn_arrival(c, j, pc).wait_recv())
        right = jnp.concatenate(
            [
                jnp.concatenate(
                    [
                        part
                        for j in range(2)
                        for part in (n_low[c, xs, j, pc], n_high[c, j, pc, xs])
                    ],
                    axis=0,
                )
                for xs, pc in groups
            ],
            axis=1,
        )
        if c < CHUNKS - 1:
            part = lax.dot_general(
                left, right, (((1,), (1,)), ((), ())), preferred_element_type=F32
            )
            if c == 0:
                acc[...] = part
            else:
                acc[...] += part
        else:
            for q in range(2):
                part = lax.dot_general(
                    left[q * 256 : (q + 1) * 256],
                    right,
                    (((1,), (1,)), ((), ())),
                    preferred_element_type=F32,
                )
                send_tiles(q, acc[q * 256 : (q + 1) * 256] + part)

    def send_tiles(q, total):
        ks = pl.ds(q * 4, 4)
        for j in range(2):
            rows = total.reshape(4, 64, 128)[:, :, j * 64 : (j + 1) * 64]
            tile = jnp.concatenate([rows[:, :32], rows[:, 32:]], axis=2).astype(BF16)
            fsend[j, ks] = tile
            mine = jnp.logical_and(own_c, y_lo == j)

            @pl.when(mine)
            def _():
                frecv[0, ks] = tile

            @pl.when(jnp.logical_not(mine))
            def _():
                f_copy(j, q).start()

    pp_load(0).wait()
    for i, d in enumerate(row_order):
        zb = (zh + d) % 4
        basis_load(zb).wait()
        project_rows(0, zb)
        if i == 0:
            pl.semaphore_wait(barrier, expected)
            for step in range(1, 4):
                for peer in (dev(y=(y + step) % 4), dev(zh=(zh + step) % 4)):
                    pl.semaphore_signal(
                        ready_sem, inc=1, device_id=peer, device_id_type=MESH
                    )
        send_y_part(0, zb)
        if d:
            zc_copy(d).start()
    pp_load(1).wait()

    def second_rows(zb, carry):
        project_rows(1, zb)
        return carry

    lax.fori_loop(0, 4, second_rows, 0, unroll=True)
    send_y(2)
    send_y(3)
    stage_y(0)
    make_weights()
    w_copy.start()
    w_copy.wait_recv()
    for d in range(1, 4):
        wx_copy(d).start()
    stage_crossed_z()
    stage_y(2)
    stage_z(0)
    stage_y(3)
    stage_crossed_y()
    stage_z(2)
    stage_relay(0)
    stage_relay(1)
    stage_m(0)
    stage_z(3)
    stage_relay(2)
    stage_response(0)
    stage_m(1)
    stage_relay(3)
    stage_response(1)
    stage_m(2)
    stage_response(2)
    stage_m(3)
    stage_response(3)
    for c in range(CHUNKS):
        for d in range(1, 4):
            if c == CROSSED:
                zc_copy(d).wait_send()
                yc_copy(d).wait_send()
            else:
                y_copy(c, d).wait_send()
                z_copy(c, d).wait_send()
            m_copy(c, d).wait_send()
            n_copy(c, d).wait_send()
            nx_copy(c, d).wait_send()
            xf_copy(c, d).wait_send()
            xn_copy(c, d).wait_send()

        @pl.when(jnp.logical_not(own_n))
        def _():
            n_copy(c, 0).wait_send()
            xn_copy(c, 0).wait_send()

        @pl.when(jnp.logical_not(own_m))
        def _():
            m_copy(c, 0).wait_send()

        relay(c).wait_send()
    w_copy.wait_send()
    for d in range(1, 4):
        wx_copy(d).wait_send()

    for q in range(2):
        ks = pl.ds(q * 4, 4)

        @pl.when(jnp.logical_not(own_c))
        def _():
            f_arrival(0, q).wait_recv()

        f_arrival(1, q).wait_recv()
        total = frecv[0, ks].astype(F32) + frecv[1, ks].astype(F32)
        rows = jnp.concatenate([total[:, :, :64], total[:, :, 64:]], axis=1)
        out_ref[ks] = jnp.swapaxes(rows, 1, 2)
    for j in range(2):
        mine = jnp.logical_and(own_c, y_lo == j)

        @pl.when(jnp.logical_not(mine))
        def _():
            for q in range(2):
                f_copy(j, q).wait_send()


def per_device(
    pair_products, basis, val_energy, cond_energy, frequencies, valence_index, conduction_index
):
    pairs_total = pair_products.shape[1] * lax.axis_size("pair")
    vmem = pl.BlockSpec(memory_space=pltpu.VMEM)
    hbm = pl.BlockSpec(memory_space=pl.ANY)
    dma = pltpu.SemaphoreType.DMA
    return pl.pallas_call(
        functools.partial(kernel, pairs_total),
        out_shape=jax.ShapeDtypeStruct((8, 64, 64), F32),
        in_specs=[hbm] * 7,
        out_specs=vmem,
        scratch_shapes=[
            pltpu.VMEM((1, 128), F32),
            pltpu.VMEM((1, 128), F32),
            pltpu.SMEM((8,), F32),
            pltpu.VMEM((1, 512), jnp.int32),
            pltpu.VMEM((1, 512), jnp.int32),
            dma((5,)),
            pltpu.SemaphoreType.REGULAR,
            pltpu.VMEM((4, 2048, 256), BF16),
            pltpu.VMEM((HALVES, 2048, 256), BF16),
            pltpu.VMEM((CHUNKS, 4, 4, 64, 128), BF16),
            pltpu.VMEM((CHUNKS, 3, 4, 64, 128), BF16),
            pltpu.VMEM((CHUNKS, 4, 64, 128), BF16),
            pltpu.VMEM((CHUNKS, 3, 64, 128), BF16),
            pltpu.VMEM((3, 4, 64, 128), BF16),
            pltpu.VMEM((4, 64, 128), BF16),
            pltpu.VMEM((3, 64, 128), BF16),
            pltpu.VMEM((CHUNKS, 64, 128), BF16),
            pltpu.VMEM((CHUNKS, 2, 4, 64, 128), BF16),
            pltpu.VMEM((CHUNKS, 4, 2, 2, HALF, 128), BF16),
            pltpu.VMEM((CHUNKS, 2, 2, 4, HALF, 128), BF16),
            pltpu.VMEM((CHUNKS, 4, HALF, 128), BF16),
            pltpu.VMEM((4, 2, CHUNKS, 8, 128), F32),
            pltpu.VMEM((512, 128), F32),
            pltpu.VMEM((2, 8, 32, 128), BF16),
            pltpu.VMEM((2, 8, 32, 128), BF16),
            dma((4,)),
            dma((HALVES,)),
            dma((CHUNKS, 3)),
            dma((CHUNKS, 3)),
            dma((CHUNKS, 3)),
            dma((CHUNKS, 3)),
            dma((CHUNKS, 4)),
            dma((CHUNKS, 4)),
            dma((CHUNKS, 4)),
            dma((CHUNKS, 4)),
            dma((CHUNKS, 3)),
            dma((CHUNKS, 3)),
            dma((CHUNKS, 3)),
            dma((CHUNKS, 3)),
            dma((CHUNKS, 4)),
            dma((CHUNKS, 4)),
            dma((CHUNKS,)),
            dma((CHUNKS,)),
            dma(()),
            dma(()),
            dma((3,)),
            dma((3,)),
            dma((2, 2)),
            dma((2, 2)),
        ],
        compiler_params=pltpu.CompilerParams(
            collective_id=0, has_side_effects=True, vmem_limit_bytes=56 * 2**20
        ),
    )(
        pair_products,
        basis,
        val_energy.reshape(1, -1),
        cond_energy.reshape(1, -1),
        frequencies,
        valence_index.reshape(1, -1),
        conduction_index.reshape(1, -1),
    )


def solution(mesh):
    placed = (P("pw", "pair"), P("pw", None), P(), P(), P(), P("pair"), P("pair"))
    return jax.shard_map(
        per_device, mesh=mesh, in_specs=placed, out_specs=P(None, "pw", "pair"), check_vma=False
    )
```

```python
import functools

import jax
import jax.numpy as jnp
from jax import lax
from jax.experimental import pallas as pl
from jax.experimental.pallas import tpu as pltpu
from jax.sharding import PartitionSpec as P

F32 = jnp.float32
BF16 = jnp.bfloat16
MESH = pl.DeviceIdType.MESH
CHUNKS = 4
CROSSED = 1
HALF = 32
HALVES = 2


def kernel(
    pairs_total,
    pp_hbm,
    basis_hbm,
    val_hbm,
    cond_hbm,
    freq_hbm,
    vidx_hbm,
    cidx_hbm,
    out_ref,
    val_ref,
    cond_ref,
    freq_ref,
    vidx_ref,
    cidx_ref,
    small_sem,
    ready_sem,
    basis_v,
    pp_v,
    psend,
    yrecv,
    zsend,
    zrecv,
    crossed_z,
    crossed_y,
    crossed_mine,
    own_rows,
    mbuf,
    n_low,
    n_high,
    over_x,
    wbuf,
    acc,
    fsend,
    frecv,
    basis_sem,
    pp_sem,
    y_ss,
    y_rs,
    z_ss,
    z_rs,
    m_ss,
    m_rs,
    n_ss,
    n_rs,
    nx_ss,
    nx_rs,
    xf_ss,
    xf_rs,
    xn_ss,
    xn_rs,
    r_ss,
    r_rs,
    w_ss,
    w_rs,
    wx_ss,
    wx_rs,
    f_ss,
    f_rs,
):
    pair, pw = lax.axis_index("pair"), lax.axis_index("pw")
    x, zl, cc = pair // 4, (pair // 2) % 2, pair % 2
    zh, y = pw // 4, pw % 4
    y_hi, y_lo = y // 2, y % 2

    def dev(x=x, zl=zl, cc=cc, zh=zh, y=y):
        return {"pair": x * 4 + zl * 2 + cc, "pw": zh * 4 + y}

    def basis_load(zb):
        return pltpu.make_async_copy(
            basis_hbm.at[:, pl.ds(pl.multiple_of(zb * 256, 256), 256)],
            basis_v.at[zb],
            basis_sem.at[zb],
        )

    def pp_load(h):
        return pltpu.make_async_copy(
            pp_hbm.at[:, pl.ds(h * 256, 256)], pp_v.at[h], pp_sem.at[h]
        )

    pp_load(0).start()
    row_order = (2, 1, 3, 0)
    for d in row_order:
        basis_load((zh + d) % 4).start()
    pp_load(1).start()
    small_loads = [
        pltpu.make_async_copy(source, target, small_sem.at[i])
        for i, (source, target) in enumerate(
            [
                (val_hbm, val_ref),
                (cond_hbm, cond_ref),
                (freq_hbm, freq_ref),
                (vidx_hbm, vidx_ref),
                (cidx_hbm, cidx_ref),
            ]
        )
    ]
    for load in small_loads:
        load.start()

    own_n = y_hi == cc
    own_m = x == zh
    own_c = jnp.logical_and(y == 2 * zl + cc, y_hi == cc)
    barrier = pltpu.get_barrier_semaphore()

    def greet(device):
        pl.semaphore_signal(barrier, inc=1, device_id=device, device_id_type=MESH)

    for d in range(1, 4):
        greet(dev(y=(y + 4 - d) % 4))
        greet(dev(zh=(zh + 4 - d) % 4))
        greet(dev(x=(x + 4 - d) % 4))
    greet(dev(cc=1 - cc))
    greet(dev(zl=1 - zl))
    expected = 11

    def y_copy(c, d):
        return pltpu.make_async_remote_copy(
            src_ref=psend.at[c, (y + d) % 4],
            dst_ref=yrecv.at[c, d - 1],
            send_sem=y_ss.at[c, d - 1],
            recv_sem=y_rs.at[c, d - 1],
            device_id=dev(y=(y + d) % 4),
            device_id_type=MESH,
        )

    def y_part(c, d, zb):
        return pltpu.make_async_remote_copy(
            src_ref=psend.at[c, (y + d) % 4, zb],
            dst_ref=yrecv.at[c, d - 1, zb],
            send_sem=y_ss.at[c, d - 1],
            recv_sem=y_rs.at[c, d - 1],
            device_id=dev(y=(y + d) % 4),
            device_id_type=MESH,
        )

    def z_copy(c, d):
        return pltpu.make_async_remote_copy(
            src_ref=zsend.at[c, (zh + d) % 4],
            dst_ref=zrecv.at[c, d - 1],
            send_sem=z_ss.at[c, d - 1],
            recv_sem=z_rs.at[c, d - 1],
            device_id=dev(zh=(zh + d) % 4),
            device_id_type=MESH,
        )

    def zc_copy(d):
        return pltpu.make_async_remote_copy(
            src_ref=psend.at[CROSSED, :, (zh + d) % 4],
            dst_ref=crossed_z.at[d - 1],
            send_sem=z_ss.at[CROSSED, d - 1],
            recv_sem=z_rs.at[CROSSED, d - 1],
            device_id=dev(zh=(zh + d) % 4),
            device_id_type=MESH,
        )

    def yc_copy(d):
        return pltpu.make_async_remote_copy(
            src_ref=crossed_y.at[(y + d) % 4],
            dst_ref=crossed_mine.at[d - 1],
            send_sem=y_ss.at[CROSSED, d - 1],
            recv_sem=y_rs.at[CROSSED, d - 1],
            device_id=dev(y=(y + d) % 4),
            device_id_type=MESH,
        )

    def m_copy(c, d):
        return pltpu.make_async_remote_copy(
            src_ref=own_rows.at[c],
            dst_ref=mbuf.at[c, cc, x],
            send_sem=m_ss.at[c, d],
            recv_sem=m_rs.at[c, x],
            device_id=dev(x=zh, zh=(zh + d) % 4),
            device_id_type=MESH,
        )

    def m_arrival(c, e):
        return pltpu.make_async_remote_copy(
            src_ref=own_rows.at[c],
            dst_ref=mbuf.at[c, cc, (x + e) % 4],
            send_sem=m_ss.at[c, 0],
            recv_sem=m_rs.at[c, (x + e) % 4],
            device_id=dev(cc=1 - cc),
            device_id_type=MESH,
        )

    low, high = pl.ds(0, HALF), pl.ds(HALF, HALF)

    def remote(source, target, send_sem, recv_sem, device):
        return pltpu.make_async_remote_copy(
            src_ref=source,
            dst_ref=target,
            send_sem=send_sem,
            recv_sem=recv_sem,
            device_id=device,
            device_id_type=MESH,
        )

    sibling = dev(cc=1 - cc)

    def n_copy(c, d):
        return remote(
            own_rows.at[c, low],
            n_low.at[c, x, y_lo, cc],
            n_ss.at[c, d],
            n_rs.at[c, y_lo * 2 + cc],
            dev(y=(y + d) % 4, cc=y_hi),
        )

    def n_arrival(c, j, pc):
        return remote(
            own_rows.at[c, low],
            n_low.at[c, x, j, pc],
            n_ss.at[c, 0],
            n_rs.at[c, j * 2 + pc],
            sibling,
        )

    def nx_copy(c, d):
        return remote(
            n_low.at[c, x],
            n_low.at[c, x],
            nx_ss.at[c, d - 1],
            nx_rs.at[c, d - 1],
            dev(x=(x + d) % 4),
        )

    def xf_copy(c, d):
        return remote(
            own_rows.at[c, high],
            over_x.at[c, x],
            xf_ss.at[c, d - 1],
            xf_rs.at[c, d - 1],
            dev(x=(x + d) % 4),
        )

    def xn_copy(c, d):
        return remote(
            over_x.at[c],
            n_high.at[c, y_lo, cc],
            xn_ss.at[c, d],
            xn_rs.at[c, y_lo * 2 + cc],
            dev(y=(y + d) % 4, cc=y_hi),
        )

    def xn_arrival(c, j, pc):
        return remote(
            over_x.at[c],
            n_high.at[c, j, pc],
            xn_ss.at[c, 0],
            xn_rs.at[c, j * 2 + pc],
            sibling,
        )

    def relay(c):
        return pltpu.make_async_remote_copy(
            src_ref=mbuf.at[c, cc],
            dst_ref=mbuf.at[c, cc],
            send_sem=r_ss.at[c],
            recv_sem=r_rs.at[c],
            device_id=dev(cc=1 - cc),
            device_id_type=MESH,
        )

    def wx_copy(d):
        return pltpu.make_async_remote_copy(
            src_ref=wbuf.at[x],
            dst_ref=wbuf.at[x],
            send_sem=wx_ss.at[d - 1],
            recv_sem=wx_rs.at[d - 1],
            device_id=dev(x=(x + d) % 4),
            device_id_type=MESH,
        )

    w_copy = pltpu.make_async_remote_copy(
        src_ref=wbuf.at[x, cc],
        dst_ref=wbuf.at[x, cc],
        send_sem=w_ss,
        recv_sem=w_rs,
        device_id=dev(cc=1 - cc),
        device_id_type=MESH,
    )

    def f_copy(j, q):
        slot = (y_hi + zl) % 2
        ks = pl.ds(q * 4, 4)
        return remote(
            fsend.at[j, ks],
            frecv.at[slot, ks],
            f_ss.at[j, q],
            f_rs.at[slot, q],
            dev(y=2 * cc + j, zl=y_hi, cc=y_lo),
        )

    def f_arrival(slot, q):
        ks = pl.ds(q * 4, 4)
        return remote(
            fsend.at[0, ks], frecv.at[slot, ks], f_ss.at[0, q], f_rs.at[slot, q], sibling
        )

    def project_rows(h, zb):
        block = lax.dot_general(
            basis_v[zb], pp_v[h], (((0,), (0,)), ((), ())), preferred_element_type=F32
        )
        block = block.astype(BF16).reshape(4, 64, 256)
        psend[2 * h, :, zb] = block[:, :, :128]
        psend[2 * h + 1, :, zb] = block[:, :, 128:]

    def send_y(c):
        for d in (2, 1, 3):
            y_copy(c, d).start()

    def send_y_part(c, zb):
        for d in (2, 1, 3):
            y_part(c, d, zb).start()

    def make_weights():
        for load in small_loads:
            load.wait()
        levels = lax.broadcasted_iota(jnp.int32, (128, 512), 0)

        def lookup(index, table):
            column = jnp.transpose(jnp.broadcast_to(table, (128, 128)))[:, :1]
            return jnp.sum(jnp.where(levels == index, column, 0.0), axis=0, keepdims=True)

        gap = lookup(cidx_ref[...], cond_ref[...]) - lookup(vidx_ref[...], val_ref[...])
        for k in range(8):
            freq = freq_ref[k]
            weight = -4.0 * gap / (gap * gap + freq * freq) / pairs_total
            for c in range(CHUNKS):
                wbuf[x, cc, c, k : k + 1, :] = weight[:, c * 128 : (c + 1) * 128]

    def stage_y(c):
        for d in range(1, 4):
            y_copy(c, d).wait_recv()
        total = psend[c, y].astype(F32)
        for d in range(3):
            total += yrecv[c, d].astype(F32)
        zsend[c] = total.astype(BF16)
        for d in (2, 1, 3):
            z_copy(c, d).start()

    def stage_z(c):
        for d in range(1, 4):
            z_copy(c, d).wait_recv()
        total = zsend[c, zh].astype(F32)
        for d in range(3):
            total += zrecv[c, d].astype(F32)
        share(c, total)

    def stage_crossed_z():
        for d in range(1, 4):
            zc_copy(d).wait_recv()
        total = psend[CROSSED, :, zh].astype(F32)
        for d in range(3):
            total += crossed_z[d].astype(F32)
        crossed_y[...] = total.astype(BF16)
        for d in (2, 1, 3):
            yc_copy(d).start()

    def stage_crossed_y():
        for d in range(1, 4):
            yc_copy(d).wait_recv()
        total = crossed_y[y].astype(F32)
        for d in range(3):
            total += crossed_mine[d].astype(F32)
        share(CROSSED, total)

    def share(c, total):
        if c == 0:
            pl.semaphore_wait(ready_sem, 6)
        own = total.astype(BF16)
        own_rows[c] = own

        @pl.when(own_m)
        def _():
            mbuf[c, cc, x] = own

        @pl.when(own_n)
        def _():
            n_low[c, x, y_lo, cc] = own[:HALF]

        over_x[c, x] = own[HALF:]
        for d in (2, 1, 3):
            n_copy(c, d).start()
            xf_copy(c, d).start()

        @pl.when(jnp.logical_not(own_n))
        def _():
            n_copy(c, 0).start()

        for d in (2, 1, 3):
            m_copy(c, d).start()

        @pl.when(jnp.logical_not(own_m))
        def _():
            m_copy(c, 0).start()

    def each_foreign(body):
        for j in range(2):
            for pc in range(2):
                mine = jnp.logical_and(own_n, jnp.logical_and(y_lo == j, cc == pc))

                @pl.when(jnp.logical_not(mine))
                def _():
                    body(j, pc)

    def stage_relay(c):
        each_foreign(lambda j, pc: n_arrival(c, j, pc).wait_recv())
        for d in (2, 1, 3):
            nx_copy(c, d).start()
        for d in range(1, 4):
            xf_copy(c, d).wait_recv()
        for d in (2, 1, 3):
            xn_copy(c, d).start()

        @pl.when(own_n)
        def _():
            n_high[c, y_lo, cc] = over_x[c]

        @pl.when(jnp.logical_not(own_n))
        def _():
            xn_copy(c, 0).start()

    def stage_m(c):
        @pl.when(jnp.logical_not(own_m))
        def _():
            m_arrival(c, 0).wait_recv()

        for e in range(1, 4):
            m_arrival(c, e).wait_recv()
        relay(c).start()

    def stage_response(c):
        if c == 0:
            for d in range(1, 4):
                wx_copy(d).wait_recv()
        relay(c).wait_recv()
        groups = [(xs, pc) for xs in range(4) for pc in range(2)]
        left = jnp.concatenate(
            [
                (wbuf[xs, pc, c][:, None, :] * mbuf[c, pc, xs].astype(F32)[None])
                .astype(BF16)
                .reshape(512, 128)
                for xs, pc in groups
            ],
            axis=1,
        )
        for d in range(1, 4):
            nx_copy(c, d).wait_recv()
        each_foreign(lambda j, pc: xn_arrival(c, j, pc).wait_recv())
        right = jnp.concatenate(
            [
                jnp.concatenate(
                    [
                        part
                        for j in range(2)
                        for part in (n_low[c, xs, j, pc], n_high[c, j, pc, xs])
                    ],
                    axis=0,
                )
                for xs, pc in groups
            ],
            axis=1,
        )
        if c < CHUNKS - 1:
            part = lax.dot_general(
                left, right, (((1,), (1,)), ((), ())), preferred_element_type=F32
            )
            if c == 0:
                acc[...] = part
            else:
                acc[...] += part
        else:
            for q in range(2):
                part = lax.dot_general(
                    left[q * 256 : (q + 1) * 256],
                    right,
                    (((1,), (1,)), ((), ())),
                    preferred_element_type=F32,
                )
                send_tiles(q, acc[q * 256 : (q + 1) * 256] + part)

    def send_tiles(q, total):
        ks = pl.ds(q * 4, 4)
        for j in range(2):
            rows = total.reshape(4, 64, 128)[:, :, j * 64 : (j + 1) * 64]
            tile = jnp.concatenate([rows[:, :32], rows[:, 32:]], axis=2).astype(BF16)
            fsend[j, ks] = tile
            mine = jnp.logical_and(own_c, y_lo == j)

            @pl.when(mine)
            def _():
                frecv[0, ks] = tile

            @pl.when(jnp.logical_not(mine))
            def _():
                f_copy(j, q).start()

    pp_load(0).wait()
    for i, d in enumerate(row_order):
        zb = (zh + d) % 4
        basis_load(zb).wait()
        project_rows(0, zb)
        if i == 0:
            pl.semaphore_wait(barrier, expected)
            for step in range(1, 4):
                for peer in (dev(y=(y + step) % 4), dev(zh=(zh + step) % 4)):
                    pl.semaphore_signal(
                        ready_sem, inc=1, device_id=peer, device_id_type=MESH
                    )
        if d:
            zc_copy(d).start()
        send_y_part(0, zb)
    pp_load(1).wait()

    def second_rows(zb, carry):
        project_rows(1, zb)
        send_y_part(2, zb)
        return carry

    lax.fori_loop(0, 4, second_rows, 0, unroll=True)
    send_y(3)
    make_weights()
    w_copy.start()
    stage_y(0)
    w_copy.wait_recv()
    for d in range(1, 4):
        wx_copy(d).start()
    stage_crossed_z()
    stage_y(2)
    stage_z(0)
    stage_y(3)
    stage_crossed_y()
    stage_z(2)
    stage_relay(0)
    stage_relay(1)
    stage_m(0)
    stage_z(3)
    stage_relay(2)
    stage_response(0)
    stage_m(1)
    stage_relay(3)
    stage_response(1)
    stage_m(2)
    stage_response(2)
    stage_m(3)
    stage_response(3)
    for c in range(CHUNKS):
        for d in range(1, 4):
            if c == CROSSED:
                zc_copy(d).wait_send()
                yc_copy(d).wait_send()
            else:
                y_copy(c, d).wait_send()
                z_copy(c, d).wait_send()
            m_copy(c, d).wait_send()
            n_copy(c, d).wait_send()
            nx_copy(c, d).wait_send()
            xf_copy(c, d).wait_send()
            xn_copy(c, d).wait_send()

        @pl.when(jnp.logical_not(own_n))
        def _():
            n_copy(c, 0).wait_send()
            xn_copy(c, 0).wait_send()

        @pl.when(jnp.logical_not(own_m))
        def _():
            m_copy(c, 0).wait_send()

        relay(c).wait_send()
    w_copy.wait_send()
    for d in range(1, 4):
        wx_copy(d).wait_send()

    for q in range(2):
        ks = pl.ds(q * 4, 4)

        @pl.when(jnp.logical_not(own_c))
        def _():
            f_arrival(0, q).wait_recv()

        f_arrival(1, q).wait_recv()
        total = frecv[0, ks].astype(F32) + frecv[1, ks].astype(F32)
        rows = jnp.concatenate([total[:, :, :64], total[:, :, 64:]], axis=1)
        out_ref[ks] = jnp.swapaxes(rows, 1, 2)
    for j in range(2):
        mine = jnp.logical_and(own_c, y_lo == j)

        @pl.when(jnp.logical_not(mine))
        def _():
            for q in range(2):
                f_copy(j, q).wait_send()


def per_device(
    pair_products, basis, val_energy, cond_energy, frequencies, valence_index, conduction_index
):
    pairs_total = pair_products.shape[1] * lax.axis_size("pair")
    vmem = pl.BlockSpec(memory_space=pltpu.VMEM)
    hbm = pl.BlockSpec(memory_space=pl.ANY)
    dma = pltpu.SemaphoreType.DMA
    return pl.pallas_call(
        functools.partial(kernel, pairs_total),
        out_shape=jax.ShapeDtypeStruct((8, 64, 64), F32),
        in_specs=[hbm] * 7,
        out_specs=vmem,
        scratch_shapes=[
            pltpu.VMEM((1, 128), F32),
            pltpu.VMEM((1, 128), F32),
            pltpu.SMEM((8,), F32),
            pltpu.VMEM((1, 512), jnp.int32),
            pltpu.VMEM((1, 512), jnp.int32),
            dma((5,)),
            pltpu.SemaphoreType.REGULAR,
            pltpu.VMEM((4, 2048, 256), BF16),
            pltpu.VMEM((HALVES, 2048, 256), BF16),
            pltpu.VMEM((CHUNKS, 4, 4, 64, 128), BF16),
            pltpu.VMEM((CHUNKS, 3, 4, 64, 128), BF16),
            pltpu.VMEM((CHUNKS, 4, 64, 128), BF16),
            pltpu.VMEM((CHUNKS, 3, 64, 128), BF16),
            pltpu.VMEM((3, 4, 64, 128), BF16),
            pltpu.VMEM((4, 64, 128), BF16),
            pltpu.VMEM((3, 64, 128), BF16),
            pltpu.VMEM((CHUNKS, 64, 128), BF16),
            pltpu.VMEM((CHUNKS, 2, 4, 64, 128), BF16),
            pltpu.VMEM((CHUNKS, 4, 2, 2, HALF, 128), BF16),
            pltpu.VMEM((CHUNKS, 2, 2, 4, HALF, 128), BF16),
            pltpu.VMEM((CHUNKS, 4, HALF, 128), BF16),
            pltpu.VMEM((4, 2, CHUNKS, 8, 128), F32),
            pltpu.VMEM((512, 128), F32),
            pltpu.VMEM((2, 8, 32, 128), BF16),
            pltpu.VMEM((2, 8, 32, 128), BF16),
            dma((4,)),
            dma((HALVES,)),
            dma((CHUNKS, 3)),
            dma((CHUNKS, 3)),
            dma((CHUNKS, 3)),
            dma((CHUNKS, 3)),
            dma((CHUNKS, 4)),
            dma((CHUNKS, 4)),
            dma((CHUNKS, 4)),
            dma((CHUNKS, 4)),
            dma((CHUNKS, 3)),
            dma((CHUNKS, 3)),
            dma((CHUNKS, 3)),
            dma((CHUNKS, 3)),
            dma((CHUNKS, 4)),
            dma((CHUNKS, 4)),
            dma((CHUNKS,)),
            dma((CHUNKS,)),
            dma(()),
            dma(()),
            dma((3,)),
            dma((3,)),
            dma((2, 2)),
            dma((2, 2)),
        ],
        compiler_params=pltpu.CompilerParams(
            collective_id=0, has_side_effects=True, vmem_limit_bytes=56 * 2**20
        ),
    )(
        pair_products,
        basis,
        val_energy.reshape(1, -1),
        cond_energy.reshape(1, -1),
        frequencies,
        valence_index.reshape(1, -1),
        conduction_index.reshape(1, -1),
    )


def solution(mesh):
    placed = (P("pw", "pair"), P("pw", None), P(), P(), P(), P("pair"), P("pair"))
    return jax.shard_map(
        per_device, mesh=mesh, in_specs=placed, out_specs=P(None, "pw", "pair"), check_vma=False
    )
```
